512 devices in a mesh: gx: 16 (over z), gy: 32 (over y, x, core).
Axes of the slice: x: 4, y: 4, z: 16, core: 2. Of those that a mesh axis runs over, the one named last changes fastest.
Arguments:
- fields: float32 [3, 2, 4096, 4096], P(None, None, 'gx', 'gy'), may hold values from -6 to 6
- pole_state: float32 [2, 2, 4096, 4096], P(None, None, 'gx', 'gy'), may hold values from -6 to 6
- stretch_state: float32 [4, 2, 4096, 4096], P(None, None, 'gx', 'gy'), may hold values from -6 to 6
- inverse_permittivity: float32 [4096, 4096], P('gx', 'gy'), may hold values from 0.3 to 1
- pole_rates: bfloat16 [3, 4096, 4096], P(None, 'gx', 'gy'), may hold values from 0.19921875 to 4
- x_profile: float32 [3, 4096], P(None, 'gx'), may hold values from 0.02 to 3, as said below
- y_profile: float32 [3, 4096], P(None, 'gy'), may hold values from 0.02 to 3, as said below
Outputs:
- next_fields: float32 [3, 2, 4096, 4096], P(None, None, 'gx', 'gy')
- next_poles: float32 [2, 2, 4096, 4096], P(None, None, 'gx', 'gy')
- next_stretch: float32 [4, 2, 4096, 4096], P(None, None, 'gx', 'gy')
The draws below stay inside these ranges and needn't reach their ends.
Inputs may be any that keep to these rules, and one draw needn't show every extreme that they name: `x_profile`: row 0 lies in 0.05 to 1, row 1 in 1 to 3, row 2 in 0.02 to 0.3. `y_profile`: row 0 lies in 0.05 to 1, row 1 in 1 to 3, row 2 in 0.02 to 0.3.
All inputs are finite; a program needn't handle non-finite values.
Results may differ from the reference program's by a relative error of at most 0.0003.
Values sent between devices are 32-bit elements; how exact they have to be, the bound alone decides.
No kernel may reach another device: no remote copies, remote signals or barrier semaphores. Data moves between devices by JAX's collectives and lax.ppermute only.
A program may use at most 64 MiB of HBM per device.

```python
import math
import jax
import jax.numpy as jnp

PLANES = 2
NX = 4096
NY = 4096


def profile_rows(key, length):
    keys = jax.random.split(key, 3)
    conduct = jnp.exp(jax.random.uniform(keys[0], (length,), jnp.float32, math.log(0.05), math.log(1.0)))
    stretch = jax.random.uniform(keys[1], (length,), jnp.float32, 1.0, 3.0)
    shift = jnp.exp(jax.random.uniform(keys[2], (length,), jnp.float32, math.log(0.02), math.log(0.3)))
    return jnp.stack([conduct, stretch, shift])


def draw_fields(key, part):
    key = jax.random.fold_in(key, 3)
    keys = jax.random.split(key, 1)
    rough = jax.random.normal(keys[0], (3, PLANES, NX, NY), jnp.float32)
    return jnp.clip(rough, -6.0, 6.0)


def draw_pole_state(key, part):
    key = jax.random.fold_in(key, 5)
    rough = jnp.clip(jax.random.normal(key, (2, PLANES, NX, NY), jnp.float32), -6.0, 6.0)
    return rough


def draw_stretch_state(key, part):
    key = jax.random.fold_in(key, 7)
    rough = jnp.clip(jax.random.normal(key, (4, PLANES, NX, NY), jnp.float32), -6.0, 6.0)
    return rough


def draw_x_profile(key, part):
    key = jax.random.fold_in(key, 11)
    return profile_rows(key, NX)


def draw_y_profile(key, part):
    key = jax.random.fold_in(key, 23)
    return profile_rows(key, NY)


def block_scale(own_key, extent, cuts, smallest, high):
    gain, own = 1.0, jax.random.fold_in(own_key, 6)
    for dim, shards_of in cuts:
        draws = jnp.exp(jax.random.uniform(jax.random.fold_in(own, dim), (shards_of,), jnp.float32, smallest / len(cuts), high / len(cuts)))
        gain = gain * jnp.repeat(draws, extent[dim] // shards_of).reshape([-1 if axis == dim else 1 for axis in range(len(extent))])
    return gain


def setup_inputs(seed: int = 0) -> dict:
    splits = jax.random.split(jax.random.key(seed), 8)
    return {
        "fields": draw_fields(jax.random.fold_in(splits[7], 71), 0),
        "pole_state": draw_pole_state(jax.random.fold_in(splits[7], 71), 0),
        "stretch_state": draw_stretch_state(jax.random.fold_in(splits[7], 71), 0),
        "inverse_permittivity": jnp.clip(0.3 + 0.7 * jax.random.uniform(splits[3], (NX, NY), jnp.float32) ** block_scale(splits[3], (NX, NY), ((0, 16), (1, 32)), -0.2, 0.2), 0.3, 1.0),
        "pole_rates": jnp.clip(jnp.exp(math.log(4.0) - 2.9996462 * jax.random.uniform(splits[4], (3, NX, NY), jnp.float32) ** block_scale(splits[4], (3, NX, NY), ((1, 16), (2, 32)), -0.2, 0.2)), 0.19921875, 4.0).astype(jnp.bfloat16),
        "x_profile": draw_x_profile(jax.random.fold_in(splits[7], 71), 0),
        "y_profile": draw_y_profile(jax.random.fold_in(splits[7], 71), 0),
    }


section_step = 0.25


def spectral(values, axis_pos):
    period = values.shape[axis_pos]
    freq_index = jnp.arange(period, dtype=jnp.int32)
    signed = jnp.where(freq_index < period // 2, freq_index, freq_index - period)
    signed = jnp.where(freq_index == period // 2, 0, signed)
    wave_vec = signed.astype(jnp.float32) * (2.0 * math.pi / period)
    layout = [1, 1, 1]
    layout[axis_pos] = period
    spectrum = jnp.fft.fft(values, axis=axis_pos) * (1j * wave_vec.reshape(layout))
    return jnp.real(jnp.fft.ifft(spectrum, axis=axis_pos)).astype(values.dtype)


def advance(fields, pole_state, stretch_state, inverse_permittivity, pole_rates, x_profile, y_profile, ez_dx, hy_dx, ez_dy, hx_dy):
    conduct_x = x_profile[0][None, :, None]
    stretch_x = x_profile[1][None, :, None]
    shift_x = x_profile[2][None, :, None]
    conduct_y = y_profile[0][None, None, :]
    stretch_y = y_profile[1][None, None, :]
    shift_y = y_profile[2][None, None, :]
    ez_x_term = ez_dx / stretch_x + stretch_state[0]
    hy_x_term = hy_dx / stretch_x + stretch_state[1]
    ez_y_term = ez_dy / stretch_y + stretch_state[2]
    hx_y_term = hx_dy / stretch_y + stretch_state[3]
    decay_x = conduct_x / stretch_x + shift_x
    decay_y = conduct_y / stretch_y + shift_y
    feed_x = conduct_x / (stretch_x * stretch_x)
    feed_y = conduct_y / (stretch_y * stretch_y)
    stretch_rate = jnp.stack([
        -decay_x * stretch_state[0] - feed_x * ez_dx,
        -decay_x * stretch_state[1] - feed_x * hy_dx,
        -decay_y * stretch_state[2] - feed_y * ez_dy,
        -decay_y * stretch_state[3] - feed_y * hx_dy])
    inverse_eps = inverse_permittivity[None]
    damping = pole_rates[0].astype(jnp.float32)[None]
    resonance = pole_rates[1].astype(jnp.float32)[None]
    plasma = pole_rates[2].astype(jnp.float32)[None]
    polar = pole_state[0]
    current = pole_state[1]
    field_rate = jnp.stack([inverse_eps * (hy_x_term - hx_y_term - current), -ez_y_term, ez_x_term])
    pole_rate = jnp.stack([current, -damping * current - resonance * polar + plasma * fields[0]])
    return (fields + section_step * field_rate, pole_state + section_step * pole_rate, stretch_state + section_step * stretch_rate)


def reference(fields, pole_state, stretch_state, inverse_permittivity, pole_rates, x_profile, y_profile):
    ez_dx = spectral(fields[0], 1)
    hy_dx = spectral(fields[2], 1)
    ez_dy = spectral(fields[0], 2)
    hx_dy = spectral(fields[1], 2)
    next_fields, next_poles, next_stretch = advance(fields, pole_state, stretch_state, inverse_permittivity, pole_rates, x_profile, y_profile, ez_dx, hy_dx, ez_dy, hx_dy)
    return next_fields, next_poles, next_stretch
```

```python
import functools
import math

import jax
import jax.numpy as jnp
import ml_dtypes
import numpy as np
from jax import lax
from jax.experimental import pallas as pl
from jax.experimental.pallas import tpu as pltpu
from jax.sharding import PartitionSpec as P

section_step = 0.25
PERIOD = 4096
BLOCKS = 16
WIDE = PERIOD // BLOCKS
RES = BLOCKS // 2 + 1
VMEM_LIMIT = 16 * 1024 * 1024


@functools.lru_cache(maxsize=None)
def circulant_blocks():
    table = np.zeros(PERIOD, np.float64)
    for n in range(1, PERIOD):
        if n != PERIOD // 2:
            sign = -1.0 if n % 2 else 1.0
            table[n] = math.pi / PERIOD * sign / math.tan(math.pi * n / PERIOD)
    row = np.arange(WIDE)
    offset = row[None, :] - row[:, None]
    return [table[(WIDE * d + offset) % PERIOD] for d in range(BLOCKS)]


def split_parts(parts):
    high = parts.astype(np.float32).astype(ml_dtypes.bfloat16)
    low = (parts - high.astype(np.float64)).astype(np.float32).astype(ml_dtypes.bfloat16)
    return np.stack([high, low], 1)


@functools.lru_cache(maxsize=None)
def residue_matrices():
    blocks = circulant_blocks()
    parts = np.zeros((RES, WIDE, 2 * WIDE), np.float64)
    for r in range(RES):
        for d in range(BLOCKS):
            turn = 2.0 * math.pi * (r * d % BLOCKS) / BLOCKS
            parts[r, :, :WIDE] += blocks[d] * (math.cos(turn) / BLOCKS)
            parts[r, :, WIDE:] -= blocks[d] * (math.sin(turn) / BLOCKS)
    return split_parts(parts)


def turned(value, turn):
    real, imag = value
    turn = turn % 1.0
    if turn == 0.0:
        return real, imag
    if turn == 0.5:
        return -real, (None if imag is None else -imag)
    if turn == 0.75:
        return imag, -real
    if turn == 0.25:
        return (None if imag is None else -imag), real
    cosine, sine = math.cos(2.0 * math.pi * turn), math.sin(2.0 * math.pi * turn)
    if imag is None:
        return real * cosine, real * sine
    return real * cosine - imag * sine, real * sine + imag * cosine


def plus(a, b):
    if b is None:
        return a
    return b if a is None else a + b


def minus(a, b):
    if b is None:
        return a
    return -b if a is None else a - b


def real_dft(values):
    count = len(values)
    if count == 2:
        return [(values[0] + values[1], None), (values[0] - values[1], None)]
    even, odd = real_dft(values[0::2]), real_dft(values[1::2])
    half, quarter = count // 2, count // 4
    result = [None] * (half + 1)
    for k in range(quarter + 1):
        spun = turned(odd[k], -k / count)
        result[k] = (plus(even[k][0], spun[0]), plus(even[k][1], spun[1]))
        mirror = (minus(even[k][0], spun[0]), minus(spun[1], even[k][1]))
        if k < quarter:
            result[half - k] = mirror
    return result


def real_inverse(spectrum):
    count = 2 * (len(spectrum) - 1)
    half, quarter = count // 2, count // 4
    if count == 2:
        return [spectrum[0][0] + spectrum[1][0], spectrum[0][0] - spectrum[1][0]]
    evens, odds = [], []
    for r in range(quarter + 1):
        low, high = spectrum[r], spectrum[half - r]
        total = (plus(low[0], high[0]), minus(low[1], high[1]))
        differ = (minus(low[0], high[0]), plus(low[1], high[1]))
        evens.append(total)
        odds.append(turned(differ, r / count))
    result = [None] * count
    result[0::2] = real_inverse(evens)
    result[1::2] = real_inverse(odds)
    return result


def forward_part(read, spectra, group, half):
    rows, lanes = pl.ds(16 * group, 16), pl.ds(128 * half, 128)
    residues = real_dft([read(p, rows, half) for p in range(BLOCKS)])
    for r, (real, imag) in enumerate(residues):
        for place, part in enumerate((real, imag)):
            if part is None:
                part = jnp.zeros_like(real)
            high = part.astype(jnp.bfloat16)
            low = (part - high.astype(jnp.float32)).astype(jnp.bfloat16)
            spectra[r, pl.ds(32 * place + 16 * group, 16), lanes] = high
            spectra[r, pl.ds(64 + 32 * place + 16 * group, 16), lanes] = low


def multiply_part(r, spectra, matrix, products):
    lines = spectra[r]
    main = jnp.dot(lines, matrix[r, 0], preferred_element_type=jnp.float32)
    rest = jnp.dot(lines[:64], matrix[r, 1], preferred_element_type=jnp.float32)
    both = main[:64] + main[64:] + rest
    products[r, 0] = both[:32, :WIDE] - both[32:, WIDE:]
    products[r, 1] = both[:32, WIDE:] + both[32:, :WIDE]


def inverse_part(write, products, group, half):
    rows, lanes = pl.ds(16 * group, 16), pl.ds(128 * half, 128)
    spectrum = []
    for r in range(RES):
        real = products[r, 0, rows, lanes]
        imag = None if r in (0, RES - 1) else products[r, 1, rows, lanes]
        spectrum.append((real, imag))
    for p, value in enumerate(real_inverse(spectrum)):
        write(p, rows, half, value)


def x_lines_kernel(lines_ref, after_ref, matrix_ref, out_ref, matrix, spectra, products, arrived):
    copies = [pltpu.make_async_copy(matrix_ref.at[r], matrix.at[r], arrived.at[r]) for r in range(RES)]
    for copy in copies:
        copy.start()

    def read(p, rows, h):
        return lines_ref[p, rows, pl.ds(128 * h, 128)]

    def write(p, rows, h, value):
        out_ref[p, rows, pl.ds(128 * h, 128)] = value

    parts = [(group, half) for group in range(2) for half in range(2)]
    for part in parts:
        forward_part(read, spectra, *part)
    for r, copy in enumerate(copies):
        copy.wait()
        multiply_part(r, spectra, matrix, products)
    for part in parts:
        inverse_part(write, products, *part)


@functools.lru_cache(maxsize=None)
def ring_matrices():
    blocks = circulant_blocks()
    parts = np.zeros((7, WIDE, 4 * WIDE), np.float64)
    for place, shift in enumerate((0, 1, 2, 3, -3, -2, -1)):
        for d in range(4):
            block = blocks[(4 * d + shift) % BLOCKS] / 4.0
            parts[place, :, :WIDE] += block
            parts[place, :, WIDE : 2 * WIDE] += block * (1 - 2 * (d % 2))
            parts[place, :, 2 * WIDE : 3 * WIDE] += 2.0 * block * (1, 0, -1, 0)[d]
            parts[place, :, 3 * WIDE :] -= 2.0 * block * (0, 1, 0, -1)[d]
    return split_parts(parts)


def y_lines_kernel(
    coords_ref, p0, p1, p2, p3, after_ref, matrix_ref, o0, o1, o2, o3, matrix, lines, sums, arrived
):
    copies = []
    for k in range(4):
        which = jnp.where(coords_ref[1] >= k, k, k + 3)
        copies.append(pltpu.make_async_copy(matrix_ref.at[which], matrix.at[k], arrived.at[k]))
    for copy in copies:
        copy.start()

    for k, piece in enumerate((p0, p1, p2, p3)):
        slot = k % 2
        for group in range(8):
            at = pl.ds(16 * group, 16)
            w0, w1, w2, w3 = (piece[i, at, :] for i in (0, 3, 2, 1))
            values = (w0 + w2 + (w1 + w3), w0 + w2 - (w1 + w3), w0 - w2, w3 - w1)
            for value, offset, gap in zip(values, (0, 256, 512, 640), (128, 128, 256, 256)):
                high = value.astype(jnp.bfloat16)
                lines[slot, pl.ds(offset + 16 * group, 16), :] = high
                low = (value - high.astype(jnp.float32)).astype(jnp.bfloat16)
                lines[slot, pl.ds(offset + gap + 16 * group, 16), :] = low
        copies[k].wait()

        def product(offset, count, columns):
            main = jnp.dot(
                lines[slot, offset : offset + 2 * count, :],
                matrix[k, 0, :, columns],
                preferred_element_type=jnp.float32,
            )
            rest = jnp.dot(
                lines[slot, offset : offset + count, :],
                matrix[k, 1, :, columns],
                preferred_element_type=jnp.float32,
            )
            return main[:count] + main[count:] + rest

        both = product(512, 256, slice(2 * WIDE, 4 * WIDE))
        terms = (
            product(0, 128, slice(0, WIDE)),
            product(256, 128, slice(WIDE, 2 * WIDE)),
            both[:128, :WIDE] - both[128:, WIDE:],
            both[:128, WIDE:] + both[128:, :WIDE],
        )
        if k == 0:
            for i, term in enumerate(terms):
                sums[i] = term
        elif k < 3:
            for i, term in enumerate(terms):
                sums[i] += term
        else:
            z0, z2, real, imag = (sums[i] + term for i, term in enumerate(terms))
            o0[...] = z0 + z2 + real
            o1[...] = z0 - z2 - imag
            o2[...] = z0 + z2 - real
            o3[...] = z0 - z2 + imag


def whole(shape):
    return pl.BlockSpec(shape, lambda *_: (0,) * len(shape))


def any_place():
    return pl.BlockSpec(memory_space=pl.ANY)


def in_hbm():
    return pl.BlockSpec(memory_space=pltpu.HBM)


def in_vmem():
    return pl.BlockSpec(memory_space=pltpu.VMEM)


def x_lines(lines, after, matrices):
    return pl.pallas_call(
        x_lines_kernel,
        in_specs=[in_vmem(), any_place(), in_hbm()],
        out_specs=in_vmem(),
        out_shape=jax.ShapeDtypeStruct((BLOCKS, 32, WIDE), jnp.float32),
        scratch_shapes=[
            pltpu.VMEM((RES, 2, WIDE, 2 * WIDE), jnp.bfloat16),
            pltpu.VMEM((RES, 128, WIDE), jnp.bfloat16),
            pltpu.VMEM((RES, 2, 32, WIDE), jnp.float32),
            pltpu.SemaphoreType.DMA((RES,)),
        ],
        cost_estimate=pl.CostEstimate(flops=900_000_000, bytes_accessed=1_000_000, transcendentals=0),
        compiler_params=pltpu.CompilerParams(vmem_limit_bytes=VMEM_LIMIT),
        name="x_lines",
    )(lines, after, matrices)


def y_lines(coords, pieces, after, matrices):
    quarter = jax.ShapeDtypeStruct((128, WIDE), jnp.float32)
    return pl.pallas_call(
        y_lines_kernel,
        in_specs=[pl.BlockSpec(memory_space=pltpu.SMEM)] + [in_vmem()] * 4 + [any_place(), in_hbm()],
        out_specs=[in_vmem()] * 4,
        out_shape=[quarter] * 4,
        scratch_shapes=[
            pltpu.VMEM((4, 2, WIDE, 4 * WIDE), jnp.bfloat16),
            pltpu.VMEM((2, 1024, WIDE), jnp.bfloat16),
            pltpu.VMEM((4, 128, WIDE), jnp.float32),
            pltpu.SemaphoreType.DMA((4,)),
        ],
        cost_estimate=pl.CostEstimate(flops=100_000_000_000, bytes_accessed=7_000_000, transcendentals=0),
        compiler_params=pltpu.CompilerParams(vmem_limit_bytes=VMEM_LIMIT),
        name="y_lines",
    )(coords, *pieces, after, matrices)


def pack_kernel(coords_ref, field_ref, x_ref, own_ref, sent_ref):
    core = coords_ref[2]
    own_rows = pl.ds(pl.multiple_of(core * 128, 128), 128)
    sent_rows = pl.ds(pl.multiple_of(128 - core * 128, 128), 128)
    for i in range(4):
        x_ref[:, 8 * i : 8 * i + 8, :] = field_ref[i // 2 * 2, i % 2].T.reshape(16, 8, 256)
        own_ref[i // 2, i % 2] = field_ref[i // 2, i % 2, own_rows, :]
        sent_ref[i // 2, i % 2] = field_ref[i // 2, i % 2, sent_rows, :]


def pack(coords, fields):
    half = jax.ShapeDtypeStruct((2, 2, 128, 128), jnp.float32)
    return pl.pallas_call(
        pack_kernel,
        in_specs=[pl.BlockSpec(memory_space=pltpu.SMEM), in_vmem()],
        out_specs=[in_vmem()] * 3,
        out_shape=[jax.ShapeDtypeStruct((16, 32, 256), jnp.float32), half, half],
        cost_estimate=pl.CostEstimate(flops=0, bytes_accessed=2_000_000, transcendentals=0),
        compiler_params=pltpu.CompilerParams(vmem_limit_bytes=VMEM_LIMIT),
        name="pack",
    )(coords, fields)


def y_pack_kernel(coords_ref, own_ref, other_ref, *out_refs):
    own_y, core = coords_ref[0], coords_ref[2]
    here = pl.ds(pl.multiple_of(core * 128, 128), 128)
    there = pl.ds(pl.multiple_of(128 - core * 128, 128), 128)
    for j in range(4):
        rows = pl.ds(pl.multiple_of(((own_y + j) & 3) * 32, 32), 32)
        for i in range(4):
            out_refs[j][32 * i : 32 * i + 32, here] = own_ref[i // 2, i % 2, rows, :]
            out_refs[j][32 * i : 32 * i + 32, there] = other_ref[i // 2, i % 2, rows, :]


def y_pack(coords, own, other):
    quarter = jax.ShapeDtypeStruct((128, WIDE), jnp.float32)
    return pl.pallas_call(
        y_pack_kernel,
        in_specs=[pl.BlockSpec(memory_space=pltpu.SMEM), in_vmem(), in_vmem()],
        out_specs=[in_vmem()] * 4,
        out_shape=[quarter] * 4,
        cost_estimate=pl.CostEstimate(flops=0, bytes_accessed=1_000_000, transcendentals=0),
        compiler_params=pltpu.CompilerParams(vmem_limit_bytes=VMEM_LIMIT),
        name="y_pack",
    )(coords, own, other)


def shifted(value, axis, distance):
    pairs = []
    for i in range(32):
        at = [i // 8, i // 2 % 4, i % 2]
        at[axis] = (at[axis] + distance) % 4
        pairs.append((i, at[0] * 8 + at[1] * 2 + at[2]))
    return lax.ppermute(value, "gy", pairs)


def other_core(value):
    return lax.ppermute(value, "gy", [(i, i ^ 1) for i in range(32)])


def ring_swap(quarters):
    moved = {j: shifted(quarters[j], 0, j) for j in (1, 3, 2)}
    return [quarters[0]] + [moved[j] for j in (1, 2, 3)]


def ring_gather(held):
    moved = {j: shifted(held, 1, j) for j in (1, 3, 2)}
    return [held] + [moved[j] for j in (1, 2, 3)]


def advance_kernel(
    coords_ref, fields, poles, stretch, inverse_eps, rates, x_prof, y_prof, x_deriv, q0, q1, q2, q3, other,
    next_fields, next_poles, next_stretch, y_deriv
):
    part, plane = pl.program_id(0), pl.program_id(1)
    own_y, core = coords_ref[0], coords_ref[2]

    @pl.when((part == 0) & (plane == 0))
    def _():
        lanes = pl.ds(pl.multiple_of(core * 128, 128), 128)
        for j, quarter in enumerate((q0, q1, q2, q3)):
            start = ((own_y - j) & 3) * 32
            own_rows = pl.ds(pl.multiple_of(core * 128 + start, 32), 32)
            other_rows = pl.ds(pl.multiple_of(128 - core * 128 + start, 32), 32)
            for i in range(4):
                y_deriv[i, own_rows, :] = quarter[32 * i : 32 * i + 32, lanes]
                y_deriv[i, other_rows, :] = other[j, 32 * i : 32 * i + 32, :]

    here = pl.ds(pl.multiple_of(part * 128, 128), 128)
    ez_dx = x_deriv[:, 0, 0].reshape(128, 128).T
    hy_dx = x_deriv[:, 1, 0].reshape(128, 128).T
    ez_dy = y_deriv[plane, here, :]
    hx_dy = y_deriv[2 + plane, here, :]
    conduct_x, stretch_x, shift_x = x_prof[:, 0:1], x_prof[:, 1:2], x_prof[:, 2:3]
    conduct_y, stretch_y, shift_y = y_prof[0:1, :], y_prof[1:2, :], y_prof[2:3, :]
    over_x, over_y = 1.0 / stretch_x, 1.0 / stretch_y
    decay_x = conduct_x / stretch_x + shift_x
    decay_y = conduct_y / stretch_y + shift_y
    feed_x = conduct_x / (stretch_x * stretch_x)
    feed_y = conduct_y / (stretch_y * stretch_y)
    s0, s1, s2, s3 = (stretch[i, 0] for i in range(4))
    ez_x_term = ez_dx * over_x + s0
    hy_x_term = hy_dx * over_x + s1
    ez_y_term = ez_dy * over_y + s2
    hx_y_term = hx_dy * over_y + s3
    next_stretch[0, 0] = s0 - section_step * (decay_x * s0 + feed_x * ez_dx)
    next_stretch[1, 0] = s1 - section_step * (decay_x * s1 + feed_x * hy_dx)
    next_stretch[2, 0] = s2 - section_step * (decay_y * s2 + feed_y * ez_dy)
    next_stretch[3, 0] = s3 - section_step * (decay_y * s3 + feed_y * hx_dy)
    polar, current = poles[0, 0], poles[1, 0]
    ez = fields[0, 0]
    next_fields[0, 0] = ez + section_step * (inverse_eps[...] * (hy_x_term - hx_y_term - current))
    next_fields[1, 0] = fields[1, 0] - section_step * ez_y_term
    next_fields[2, 0] = fields[2, 0] + section_step * ez_x_term
    damping, resonance, plasma = (rates[i].astype(jnp.float32) for i in range(3))
    next_poles[0, 0] = polar + section_step * current
    next_poles[1, 0] = current + section_step * (plasma * ez - damping * current - resonance * polar)


def advance(coords, fields, pole_state, stretch_state, inverse_permittivity, pole_rates, x_profile, y_profile, x_deriv, quarters, other):
    def state(count):
        return pl.BlockSpec((count, 1, 128, 128), lambda i, j, *_: (0, j, i, 0))

    return pl.pallas_call(
        advance_kernel,
        grid_spec=pltpu.PrefetchScalarGridSpec(
            num_scalar_prefetch=1,
            grid=(2, 2),
            in_specs=[
                state(3),
                state(2),
                state(4),
                pl.BlockSpec((128, 128), lambda i, j, *_: (i, 0)),
                pl.BlockSpec((3, 128, 128), lambda i, j, *_: (0, i, 0)),
                pl.BlockSpec((128, 3), lambda i, j, *_: (i, 0)),
                whole((3, 128)),
                pl.BlockSpec((16, 2, 1, 8, 128), lambda i, j, *_: (0, 0, j, 0, i)),
            ]
            + [whole((128, WIDE))] * 4
            + [whole((4, 128, 128))],
            out_specs=[state(3), state(2), state(4)],
            scratch_shapes=[pltpu.VMEM((4, 256, 128), jnp.float32)],
        ),
        out_shape=[
            jax.ShapeDtypeStruct((count, 2, 256, 128), jnp.float32) for count in (3, 2, 4)
        ],
        cost_estimate=pl.CostEstimate(flops=3_000_000, bytes_accessed=6_000_000, transcendentals=0),
        compiler_params=pltpu.CompilerParams(vmem_limit_bytes=VMEM_LIMIT),
        name="advance",
    )(coords, fields, pole_state, stretch_state, inverse_permittivity, pole_rates, x_profile.T, y_profile,
        x_deriv.reshape(16, 2, 2, 8, 256), *quarters, other)


def swap_x(lines):
    return lax.all_to_all(lines, "gx", split_axis=0, concat_axis=0, tiled=True)


def y_return(coords, quarters):
    quarters = ring_swap(quarters)
    core = coords[2]
    sent = jnp.stack([lax.dynamic_slice_in_dim(q, 128 - core * 128, 128, 1) for q in quarters])
    return quarters, other_core(sent)


def place():
    me = lax.axis_index("gy").astype(jnp.int32)
    return jnp.stack([me // 8, me // 2 % 4, me % 2])


def shards(fields, pole_state, stretch_state, inverse_permittivity, pole_rates, x_profile, y_profile):
    coords = place()
    x_mats, y_mats = jnp.asarray(residue_matrices()), jnp.asarray(ring_matrices())
    x_packed, own, sent = pack(coords, fields)
    x_sorted = swap_x(x_packed)
    y_held = jnp.stack(ring_swap(y_pack(coords, own, other_core(sent))))
    y_pieces = ring_gather(y_held)
    x_lined = x_lines(x_sorted, y_held, x_mats)
    x_deriv = swap_x(x_lined)
    quarters, other = y_return(coords, y_lines(coords, y_pieces, x_lined, y_mats))
    return tuple(
        advance(
            coords, fields, pole_state, stretch_state, inverse_permittivity, pole_rates, x_profile, y_profile,
            x_deriv, quarters, other,
        )
    )


def solution(mesh):
    return jax.shard_map(
        shards,
        mesh=mesh,
        in_specs=(
            P(None, None, "gx", "gy"),
            P(None, None, "gx", "gy"),
            P(None, None, "gx", "gy"),
            P("gx", "gy"),
            P(None, "gx", "gy"),
            P(None, "gx"),
            P(None, "gy"),
        ),
        out_specs=(P(None, None, "gx", "gy"), P(None, None, "gx", "gy"), P(None, None, "gx", "gy")),
        check_vma=False,
    )
```

```python
import functools
import math

import jax
import jax.numpy as jnp
import ml_dtypes
import numpy as np
from jax import lax
from jax.experimental import pallas as pl
from jax.experimental.pallas import tpu as pltpu
from jax.sharding import PartitionSpec as P

section_step = 0.25
PERIOD = 4096
BLOCKS = 16
WIDE = PERIOD // BLOCKS
RES = BLOCKS // 2 + 1
VMEM_LIMIT = 16 * 1024 * 1024
VMEM_MOST = 49 * 1024 * 1024


@functools.lru_cache(maxsize=None)
def circulant_blocks():
    table = np.zeros(PERIOD, np.float64)
    for n in range(1, PERIOD):
        if n != PERIOD // 2:
            sign = -1.0 if n % 2 else 1.0
            table[n] = math.pi / PERIOD * sign / math.tan(math.pi * n / PERIOD)
    row = np.arange(WIDE)
    offset = row[None, :] - row[:, None]
    return [table[(WIDE * d + offset) % PERIOD] for d in range(BLOCKS)]


def split_parts(parts):
    high = parts.astype(np.float32).astype(ml_dtypes.bfloat16)
    low = (parts - high.astype(np.float64)).astype(np.float32).astype(ml_dtypes.bfloat16)
    return np.stack([high, low], 1)


@functools.lru_cache(maxsize=None)
def residue_tables():
    dft = np.zeros((1, WIDE, 2 * WIDE), np.float64)
    cosines = [math.cos(2.0 * math.pi * n / WIDE) for n in range(WIDE)]
    sines = [math.sin(2.0 * math.pi * n / WIDE) for n in range(WIDE)]
    row = np.arange(WIDE)
    product = row[:, None] * row[None, :] % WIDE
    dft[0, :, :WIDE] = np.array(cosines)[product]
    dft[0, :, WIDE:] = -np.array(sines)[product]
    vectors = np.zeros((3, RES, WIDE), np.float64)
    for r in range(RES):
        for m in range(WIDE):
            turn = 2.0 * math.pi * (r * m) / PERIOD
            vectors[0, r, m], vectors[1, r, m] = math.cos(turn), math.sin(turn)
            freq = r + BLOCKS * m
            signed = freq if freq < PERIOD // 2 else freq - PERIOD
            if freq != PERIOD // 2:
                vectors[2, r, m] = 2.0 * math.pi * signed / PERIOD / PERIOD
    return split_parts(dft)[0], vectors.astype(np.float32)


def turned(value, turn):
    real, imag = value
    turn = turn % 1.0
    if turn == 0.0:
        return real, imag
    if turn == 0.5:
        return -real, (None if imag is None else -imag)
    if turn == 0.75:
        return imag, -real
    if turn == 0.25:
        return (None if imag is None else -imag), real
    cosine, sine = math.cos(2.0 * math.pi * turn), math.sin(2.0 * math.pi * turn)
    if imag is None:
        return real * cosine, real * sine
    return real * cosine - imag * sine, real * sine + imag * cosine


def plus(a, b):
    if b is None:
        return a
    return b if a is None else a + b


def minus(a, b):
    if b is None:
        return a
    return -b if a is None else a - b


def real_dft(values):
    count = len(values)
    if count == 2:
        return [(values[0] + values[1], None), (values[0] - values[1], None)]
    even, odd = real_dft(values[0::2]), real_dft(values[1::2])
    half, quarter = count // 2, count // 4
    result = [None] * (half + 1)
    for k in range(quarter + 1):
        spun = turned(odd[k], -k / count)
        result[k] = (plus(even[k][0], spun[0]), plus(even[k][1], spun[1]))
        mirror = (minus(even[k][0], spun[0]), minus(spun[1], even[k][1]))
        if k < quarter:
            result[half - k] = mirror
    return result


def real_inverse(spectrum):
    count = 2 * (len(spectrum) - 1)
    half, quarter = count // 2, count // 4
    if count == 2:
        return [spectrum[0][0] + spectrum[1][0], spectrum[0][0] - spectrum[1][0]]
    evens, odds = [], []
    for r in range(quarter + 1):
        low, high = spectrum[r], spectrum[half - r]
        total = (plus(low[0], high[0]), minus(low[1], high[1]))
        differ = (minus(low[0], high[0]), plus(low[1], high[1]))
        evens.append(total)
        odds.append(turned(differ, r / count))
    result = [None] * count
    result[0::2] = real_inverse(evens)
    result[1::2] = real_inverse(odds)
    return result


def store_split(target, first, second, value):
    high = value.astype(jnp.bfloat16)
    target[first] = high
    target[second] = (value - high.astype(jnp.float32)).astype(jnp.bfloat16)


def wide_product(lines, matrix):
    half = lines.shape[0] // 2
    main = jnp.dot(lines[...], matrix[0], preferred_element_type=jnp.float32)
    rest = jnp.dot(lines[:half], matrix[1], preferred_element_type=jnp.float32)
    both = main[:half] + main[half:] + rest
    quarter = half // 2
    return both[:quarter, :WIDE], both[:quarter, WIDE:], both[quarter:, :WIDE], both[quarter:, WIDE:]


def residue_part(some, residues, lines, matrix, vectors):
    def put(i, place, value):
        store_split(
            lines, pl.ds(96 * place + 32 * i, 32), pl.ds(192 + 96 * place + 32 * i, 32), value
        )

    for i, r in enumerate(some):
        cosine, sine = vectors[0, r : r + 1], vectors[1, r : r + 1]
        real, imag = residues[r, 0], residues[r, 1]
        put(i, 0, real * cosine + imag * sine)
        put(i, 1, imag * cosine - real * sine)
    rc, rs, ic, is_ = wide_product(lines, matrix)
    real, imag = rc - is_, rs + ic
    for i, r in enumerate(some):
        wave, at = vectors[2, r : r + 1], slice(32 * i, 32 * i + 32)
        put(i, 0, -wave * imag[at])
        put(i, 1, wave * real[at])
    rc, rs, ic, is_ = wide_product(lines, matrix)
    real, imag = rc + is_, ic - rs
    for i, r in enumerate(some):
        cosine, sine = vectors[0, r : r + 1], vectors[1, r : r + 1]
        at = slice(32 * i, 32 * i + 32)
        residues[r, 0] = real[at] * cosine - imag[at] * sine
        residues[r, 1] = real[at] * sine + imag[at] * cosine


def x_lines_kernel(lines_ref, after_ref, matrix, vectors, out_ref, work, residues, lines, arrived, sent):
    parts = [(pl.ds(16 * g, 16), pl.ds(128 * h, 128)) for g in range(2) for h in range(2)]
    incoming, outgoing = [], []
    for i, (rows, lanes) in enumerate(parts):
        here = (slice(None), rows, lanes)
        incoming.append(pltpu.make_async_copy(lines_ref.at[here], work.at[here], arrived.at[i]))
        outgoing.append(pltpu.make_async_copy(work.at[here], out_ref.at[here], sent.at[i]))
        incoming[-1].start()
    for copy, (rows, lanes) in zip(incoming, parts):
        copy.wait()
        for r, (real, imag) in enumerate(real_dft([work[p, rows, lanes] for p in range(BLOCKS)])):
            residues[r, 0, rows, lanes] = real
            residues[r, 1, rows, lanes] = jnp.zeros_like(real) if imag is None else imag
    for first in range(0, RES, 3):
        residue_part(range(first, first + 3), residues, lines, matrix, vectors)
    for copy, (rows, lanes) in zip(outgoing, parts):
        spectrum = []
        for r in range(RES):
            imag = None if r in (0, RES - 1) else residues[r, 1, rows, lanes]
            spectrum.append((residues[r, 0, rows, lanes], imag))
        for p, value in enumerate(real_inverse(spectrum)):
            work[p, rows, lanes] = value
        copy.start()
    for copy in outgoing:
        copy.wait()


@functools.lru_cache(maxsize=None)
def ring_matrices():
    blocks = circulant_blocks()
    parts = np.zeros((16, WIDE, 4 * WIDE), np.float64)
    for own in range(4):
        for k in range(4):
            place = 4 * own + k
            for d in range(4):
                block = blocks[(4 * d + own - (own - k) % 4) % BLOCKS] / 4.0
                parts[place, :, :WIDE] += block
                parts[place, :, WIDE : 2 * WIDE] += block * (1 - 2 * (d % 2))
                parts[place, :, 2 * WIDE : 3 * WIDE] += 2.0 * block * (1, 0, -1, 0)[d]
                parts[place, :, 3 * WIDE :] -= 2.0 * block * (0, 1, 0, -1)[d]
    return split_parts(parts)


def y_lines_kernel(me_ref, p0, p1, p2, p3, after_ref, matrix_ref, o0, o1, o2, o3, matrix, lines, sums, arrived):
    first = 4 * ((me_ref[0] >> 1) & 3)
    copies = [pltpu.make_async_copy(matrix_ref.at[first + k], matrix.at[k], arrived.at[k]) for k in range(4)]
    for copy in copies:
        copy.start()

    for k, piece in enumerate((p0, p1, p2, p3)):
        slot = k % 2
        for group in range(8):
            at = pl.ds(16 * group, 16)
            w0, w1, w2, w3 = (piece[i, at, :] for i in (0, 3, 2, 1))
            values = (w0 + w2 + (w1 + w3), w0 + w2 - (w1 + w3), w0 - w2, w3 - w1)
            for value, offset, gap in zip(values, (0, 256, 512, 640), (128, 128, 256, 256)):
                high = value.astype(jnp.bfloat16)
                lines[slot, pl.ds(offset + 16 * group, 16), :] = high
                low = (value - high.astype(jnp.float32)).astype(jnp.bfloat16)
                lines[slot, pl.ds(offset + gap + 16 * group, 16), :] = low
        copies[k].wait()

        def product(offset, count, columns):
            main = jnp.dot(
                lines[slot, offset : offset + 2 * count, :],
                matrix[k, 0, :, columns],
                preferred_element_type=jnp.float32,
            )
            rest = jnp.dot(
                lines[slot, offset : offset + count, :],
                matrix[k, 1, :, columns],
                preferred_element_type=jnp.float32,
            )
            return main[:count] + main[count:] + rest

        both = product(512, 256, slice(2 * WIDE, 4 * WIDE))
        terms = (
            product(0, 128, slice(0, WIDE)),
            product(256, 128, slice(WIDE, 2 * WIDE)),
            both[:128, :WIDE] - both[128:, WIDE:],
            both[:128, WIDE:] + both[128:, :WIDE],
        )
        if k == 0:
            for i, term in enumerate(terms):
                sums[i] = term
        elif k < 3:
            for i, term in enumerate(terms):
                sums[i] += term
        else:
            z0, z2, real, imag = (sums[i] + term for i, term in enumerate(terms))
            o0[...] = z0 + z2 + real
            o1[...] = z0 - z2 - imag
            o2[...] = z0 + z2 - real
            o3[...] = z0 - z2 + imag


def whole(shape):
    return pl.BlockSpec(shape, lambda *_: (0,) * len(shape))


def any_place():
    return pl.BlockSpec(memory_space=pl.ANY)


def in_hbm():
    return pl.BlockSpec(memory_space=pltpu.HBM)


def in_vmem():
    return pl.BlockSpec(memory_space=pltpu.VMEM)


def in_smem():
    return pl.BlockSpec(memory_space=pltpu.SMEM)


def x_lines(lines, after):
    matrix, vectors = residue_tables()
    return pl.pallas_call(
        x_lines_kernel,
        in_specs=[any_place(), any_place(), in_vmem(), in_vmem()],
        out_specs=any_place(),
        out_shape=jax.ShapeDtypeStruct((BLOCKS, 32, WIDE), jnp.float32),
        scratch_shapes=[
            pltpu.VMEM((BLOCKS, 32, WIDE), jnp.float32),
            pltpu.VMEM((RES, 2, 32, WIDE), jnp.float32),
            pltpu.VMEM((384, WIDE), jnp.bfloat16),
            pltpu.SemaphoreType.DMA((4,)),
            pltpu.SemaphoreType.DMA((4,)),
        ],
        cost_estimate=pl.CostEstimate(flops=900_000_000, bytes_accessed=1_000_000, transcendentals=0),
        compiler_params=pltpu.CompilerParams(vmem_limit_bytes=VMEM_LIMIT),
        name="x_lines",
    )(lines, after, jnp.asarray(matrix), jnp.asarray(vectors))


def y_lines(me, pieces, after):
    quarter = jax.ShapeDtypeStruct((128, WIDE), jnp.float32)
    return pl.pallas_call(
        y_lines_kernel,
        in_specs=[in_smem()] + [in_vmem()] * 4 + [any_place(), in_hbm()],
        out_specs=[in_vmem()] * 4,
        out_shape=[quarter] * 4,
        scratch_shapes=[
            pltpu.VMEM((4, 2, WIDE, 4 * WIDE), jnp.bfloat16),
            pltpu.VMEM((2, 1024, WIDE), jnp.bfloat16),
            pltpu.VMEM((4, 128, WIDE), jnp.float32),
            pltpu.SemaphoreType.DMA((4,)),
        ],
        cost_estimate=pl.CostEstimate(flops=100_000_000_000, bytes_accessed=7_000_000, transcendentals=0),
        compiler_params=pltpu.CompilerParams(vmem_limit_bytes=VMEM_MOST),
        name="y_lines",
    )(me, *pieces, after, jnp.asarray(ring_matrices()))


def pack_kernel(me_ref, fields, x_ref, own_ref, sent_ref, lines, arrived):
    core = me_ref[0] & 1
    own_rows = pl.ds(pl.multiple_of(core * 128, 128), 128)
    sent_rows = pl.ds(pl.multiple_of(128 - core * 128, 128), 128)
    copies = []
    for i in range(4):
        at = (slice(None), pl.ds(8 * i, 8))
        lines[at] = fields[i // 2 * 2, i % 2].T.reshape(16, 8, 256)
        copies.append(pltpu.make_async_copy(lines.at[at], x_ref.at[at], arrived.at[i]))
        copies[-1].start()
    for i in range(4):
        own_ref[i // 2, i % 2] = fields[i // 2, i % 2, own_rows, :]
        sent_ref[i // 2, i % 2] = fields[i // 2, i % 2, sent_rows, :]
    for copy in copies:
        copy.wait()


def pack(me, fields):
    half = jax.ShapeDtypeStruct((2, 2, 128, 128), jnp.float32)
    return pl.pallas_call(
        pack_kernel,
        in_specs=[in_smem(), in_vmem()],
        out_specs=[any_place(), in_vmem(), in_vmem()],
        out_shape=[jax.ShapeDtypeStruct((16, 32, 256), jnp.float32), half, half],
        scratch_shapes=[pltpu.VMEM((16, 32, 256), jnp.float32), pltpu.SemaphoreType.DMA((4,))],
        cost_estimate=pl.CostEstimate(flops=0, bytes_accessed=2_000_000, transcendentals=0),
        compiler_params=pltpu.CompilerParams(vmem_limit_bytes=VMEM_LIMIT),
        name="pack",
    )(me, fields)


def y_pack_kernel(me_ref, own_ref, other_ref, *out_refs):
    own_y, core = me_ref[0] >> 3, me_ref[0] & 1
    here = pl.ds(pl.multiple_of(core * 128, 128), 128)
    there = pl.ds(pl.multiple_of(128 - core * 128, 128), 128)
    for j in range(4):
        rows = pl.ds(pl.multiple_of(((own_y + j) & 3) * 32, 32), 32)
        for i in range(4):
            out_refs[j][32 * i : 32 * i + 32, here] = own_ref[i // 2, i % 2, rows, :]
            out_refs[j][32 * i : 32 * i + 32, there] = other_ref[i // 2, i % 2, rows, :]


def y_pack(me, own, other):
    quarter = jax.ShapeDtypeStruct((128, WIDE), jnp.float32)
    return pl.pallas_call(
        y_pack_kernel,
        in_specs=[in_smem(), in_vmem(), in_vmem()],
        out_specs=[in_vmem()] * 4,
        out_shape=[quarter] * 4,
        cost_estimate=pl.CostEstimate(flops=100_000_000_000, bytes_accessed=1_000_000, transcendentals=0),
        compiler_params=pltpu.CompilerParams(vmem_limit_bytes=VMEM_LIMIT),
        name="y_pack",
    )(me, own, other)


def shifted(value, axis, distance):
    pairs = []
    for i in range(32):
        at = [i // 8, i // 2 % 4, i % 2]
        at[axis] = (at[axis] + distance) % 4
        pairs.append((i, at[0] * 8 + at[1] * 2 + at[2]))
    return lax.ppermute(value, "gy", pairs)


def other_core(value):
    return lax.ppermute(value, "gy", [(i, i ^ 1) for i in range(32)])


def ring_swap(quarters):
    moved = {j: shifted(quarters[j], 0, j) for j in (1, 3, 2)}
    return [quarters[0]] + [moved[j] for j in (1, 2, 3)]


def ring_gather(held):
    moved = {j: shifted(held, 1, j) for j in (1, 3, 2)}
    return [held] + [moved[j] for j in (1, 2, 3)]


def base_kernel(
    fields_ref, poles_ref, stretch_ref, eps_ref, rates_ref, x_prof, y_prof, after_ref,
    next_poles, base, scale, vectors, fields, poles, stretch, inverse_eps, rates, out, arrived, sent
):
    pairs = [(poles_ref, poles), (rates_ref, rates), (fields_ref, fields), (eps_ref, inverse_eps), (stretch_ref, stretch)]
    copies = [pltpu.make_async_copy(a, b, arrived.at[k]) for k, (a, b) in enumerate(pairs)]
    for copy in copies:
        copy.start()
    conduct_x, stretch_x, shift_x = x_prof[0:1, :], x_prof[1:2, :], x_prof[2:3, :]
    conduct_y, stretch_y, shift_y = y_prof[0:1, :], y_prof[1:2, :], y_prof[2:3, :]
    decay_y = conduct_y / stretch_y + shift_y

    def down(row):
        return jnp.broadcast_to(row, (128, 256)).T

    decay_x = down(conduct_x / stretch_x + shift_x)
    vectors[0:1, :] = 1.0 / stretch_x
    vectors[1:2, :] = section_step * conduct_x / (stretch_x * stretch_x)
    vectors[2:3, 0:128] = 1.0 / stretch_y
    vectors[3:4, 0:128] = section_step * conduct_y / (stretch_y * stretch_y)
    for copy in copies[:3]:
        copy.wait()
    for plane in range(2):
        polar, current, ez = poles[0, plane], poles[1, plane], fields[0, plane]
        damping, resonance, plasma = (rates[i].astype(jnp.float32) for i in range(3))
        out[0, plane] = polar + section_step * current
        out[1, plane] = current + section_step * (plasma * ez - damping * current - resonance * polar)
    result = pltpu.make_async_copy(out, next_poles, sent)
    result.start()
    for copy in copies[3:]:
        copy.wait()
    eps = section_step * inverse_eps[...]
    scale[...] = eps
    for plane in range(2):
        s0, s1, s2, s3 = (stretch[i, plane] for i in range(4))
        base[0, plane] = fields[0, plane] + eps * (s1 - s3 - poles[1, plane])
        base[1, plane] = fields[1, plane] - section_step * s2
        base[2, plane] = fields[2, plane] + section_step * s0
        base[3, plane] = s0 - section_step * (decay_x * s0)
        base[4, plane] = s1 - section_step * (decay_x * s1)
        base[5, plane] = s2 - section_step * (decay_y * s2)
        base[6, plane] = s3 - section_step * (decay_y * s3)
    result.wait()


def base_part(fields, pole_state, stretch_state, inverse_permittivity, pole_rates, x_profile, y_profile, after):
    return pl.pallas_call(
        base_kernel,
        in_specs=[any_place()] * 5 + [in_vmem()] * 2 + [any_place()],
        out_specs=[in_hbm(), in_vmem(), in_vmem(), in_vmem()],
        out_shape=[
            jax.ShapeDtypeStruct((2, 2, 256, 128), jnp.float32),
            jax.ShapeDtypeStruct((7, 2, 256, 128), jnp.float32),
            jax.ShapeDtypeStruct((256, 128), jnp.float32),
            jax.ShapeDtypeStruct((8, 256), jnp.float32),
        ],
        scratch_shapes=[
            pltpu.VMEM((3, 2, 256, 128), jnp.float32),
            pltpu.VMEM((2, 2, 256, 128), jnp.float32),
            pltpu.VMEM((4, 2, 256, 128), jnp.float32),
            pltpu.VMEM((256, 128), jnp.float32),
            pltpu.VMEM((3, 256, 128), jnp.bfloat16),
            pltpu.VMEM((2, 2, 256, 128), jnp.float32),
            pltpu.SemaphoreType.DMA((5,)),
            pltpu.SemaphoreType.DMA,
        ],
        cost_estimate=pl.CostEstimate(flops=3_000_000, bytes_accessed=5_000_000, transcendentals=0),
        compiler_params=pltpu.CompilerParams(vmem_limit_bytes=VMEM_LIMIT),
        name="base",
    )(fields, pole_state, stretch_state, inverse_permittivity, pole_rates, x_profile, y_profile, after)


def finish_kernel(
    me_ref, base, scale, vectors, x_deriv, q0, q1, q2, q3, other, next_fields, next_stretch, y_deriv, fields, stretch, sent
):
    own_y, core = me_ref[0] >> 3, me_ref[0] & 1
    lanes = pl.ds(pl.multiple_of(core * 128, 128), 128)
    for j, quarter in enumerate((q0, q1, q2, q3)):
        start = ((own_y - j) & 3) * 32
        own_rows = pl.ds(pl.multiple_of(core * 128 + start, 32), 32)
        other_rows = pl.ds(pl.multiple_of(128 - core * 128 + start, 32), 32)
        for i in range(4):
            y_deriv[i, own_rows, :] = quarter[32 * i : 32 * i + 32, lanes]
            y_deriv[i, other_rows, :] = other[j, 32 * i : 32 * i + 32, :]
    over_y, feed_y = vectors[2:3, 0:128], vectors[3:4, 0:128]
    over_x, feed_x = (jnp.broadcast_to(vectors[i : i + 1, :], (128, 256)).T for i in range(2))
    eps = scale[...]
    copies = []

    def send(source, target):
        copy = pltpu.make_async_copy(source, target, sent.at[len(copies)])
        copy.start()
        copies.append(copy)

    for plane in range(2):
        ez_dy, hx_dy = y_deriv[plane], y_deriv[2 + plane]
        stretch[2, plane] = base[5, plane] - feed_y * ez_dy
        stretch[3, plane] = base[6, plane] - feed_y * hx_dy
        fields[1, plane] = base[1, plane] - section_step * (over_y * ez_dy)
        send(stretch.at[pl.ds(2, 2), plane], next_stretch.at[pl.ds(2, 2), plane])
        send(fields.at[1, plane], next_fields.at[1, plane])
    for plane in range(2):
        ez_dx = x_deriv[:, 8 * plane : 8 * plane + 8, :].reshape(128, 256).T
        hy_dx = x_deriv[:, 16 + 8 * plane : 24 + 8 * plane, :].reshape(128, 256).T
        stretch[0, plane] = base[3, plane] - feed_x * ez_dx
        stretch[1, plane] = base[4, plane] - feed_x * hy_dx
        fields[2, plane] = base[2, plane] + section_step * (over_x * ez_dx)
        fields[0, plane] = base[0, plane] + eps * (over_x * hy_dx - over_y * y_deriv[2 + plane])
        send(stretch.at[pl.ds(0, 2), plane], next_stretch.at[pl.ds(0, 2), plane])
        send(fields.at[2, plane], next_fields.at[2, plane])
        send(fields.at[0, plane], next_fields.at[0, plane])
    for copy in copies:
        copy.wait()


def finish(me, base, scale, vectors, x_deriv, quarters, other):
    return pl.pallas_call(
        finish_kernel,
        in_specs=[in_smem()] + [in_vmem()] * 9,
        out_specs=[in_hbm()] * 2,
        out_shape=[jax.ShapeDtypeStruct((count, 2, 256, 128), jnp.float32) for count in (3, 4)],
        scratch_shapes=[
            pltpu.VMEM((4, 256, 128), jnp.float32),
            pltpu.VMEM((3, 2, 256, 128), jnp.float32),
            pltpu.VMEM((4, 2, 256, 128), jnp.float32),
            pltpu.SemaphoreType.DMA((10,)),
        ],
        cost_estimate=pl.CostEstimate(flops=3_000_000, bytes_accessed=5_000_000, transcendentals=0),
        compiler_params=pltpu.CompilerParams(vmem_limit_bytes=VMEM_LIMIT),
        name="finish",
    )(me, base, scale, vectors, x_deriv, *quarters, other)


def swap_x(lines):
    return lax.all_to_all(lines, "gx", split_axis=0, concat_axis=0, tiled=True)


def split_kernel(me_ref, q0, q1, q2, q3, after_ref, sent_ref):
    lanes = pl.ds(pl.multiple_of(128 - (me_ref[0] & 1) * 128, 128), 128)
    for j, quarter in enumerate((q0, q1, q2, q3)):
        sent_ref[j] = quarter[:, lanes]


def split(me, quarters, after):
    return pl.pallas_call(
        split_kernel,
        in_specs=[in_smem()] + [in_vmem()] * 4 + [any_place()],
        out_specs=in_vmem(),
        out_shape=jax.ShapeDtypeStruct((4, 128, 128), jnp.float32),
        cost_estimate=pl.CostEstimate(flops=0, bytes_accessed=500_000, transcendentals=0),
        compiler_params=pltpu.CompilerParams(vmem_limit_bytes=VMEM_LIMIT),
        name="split",
    )(me, *quarters, after)


def shards(fields, pole_state, stretch_state, inverse_permittivity, pole_rates, x_profile, y_profile):
    me = lax.axis_index("gy").astype(jnp.int32).reshape(1)
    x_packed, own, sent = pack(me, fields)
    x_sorted = swap_x(x_packed)
    y_packed = y_pack(me, own, other_core(sent))
    y_held = jnp.stack(ring_swap(y_packed))
    y_pieces = ring_gather(y_held)
    x_lined = x_lines(x_sorted, y_held)
    x_deriv = swap_x(x_lined)
    y_lined = y_lines(me, y_pieces, x_lined)
    next_poles, base, scale, vectors = base_part(
        fields, pole_state, stretch_state, inverse_permittivity, pole_rates, x_profile, y_profile, y_lined[0]
    )
    quarters = ring_swap(y_lined)
    other = other_core(split(me, quarters, vectors))
    next_fields, next_stretch = finish(me, base, scale, vectors, x_deriv, quarters, other)
    return next_fields, next_poles, next_stretch


def solution(mesh):
    return jax.shard_map(
        shards,
        mesh=mesh,
        in_specs=(
            P(None, None, "gx", "gy"),
            P(None, None, "gx", "gy"),
            P(None, None, "gx", "gy"),
            P("gx", "gy"),
            P(None, "gx", "gy"),
            P(None, "gx"),
            P(None, "gy"),
        ),
        out_specs=(P(None, None, "gx", "gy"), P(None, None, "gx", "gy"), P(None, None, "gx", "gy")),
        check_vma=False,
    )
```

```python
import functools
import math

import jax
import jax.numpy as jnp
import ml_dtypes
import numpy as np
from jax import lax
from jax.experimental import pallas as pl
from jax.experimental.pallas import tpu as pltpu
from jax.sharding import PartitionSpec as P

section_step = 0.25
PERIOD = 4096
BLOCKS = 16
WIDE = PERIOD // BLOCKS
RES = BLOCKS // 2 + 1
RING = (0, 1, 3, 5, 7, 9, 11, 13, 15, 14, 12, 10, 8, 6, 4, 2)
PLACE = tuple(RING.index(p) for p in range(BLOCKS))
VMEM_LIMIT = 16 * 1024 * 1024
VMEM_MOST = 49 * 1024 * 1024


@functools.lru_cache(maxsize=None)
def circulant_blocks():
    table = np.zeros(PERIOD, np.float64)
    for n in range(1, PERIOD):
        if n != PERIOD // 2:
            sign = -1.0 if n % 2 else 1.0
            table[n] = math.pi / PERIOD * sign / math.tan(math.pi * n / PERIOD)
    row = np.arange(WIDE)
    offset = row[None, :] - row[:, None]
    return [table[(WIDE * d + offset) % PERIOD] for d in range(BLOCKS)]


def split_parts(parts):
    high = parts.astype(np.float32).astype(ml_dtypes.bfloat16)
    low = (parts - high.astype(np.float64)).astype(np.float32).astype(ml_dtypes.bfloat16)
    return np.stack([high, low], 1)


@functools.lru_cache(maxsize=None)
def residue_tables():
    dft = np.zeros((1, WIDE, 2 * WIDE), np.float64)
    cosines = [math.cos(2.0 * math.pi * n / WIDE) for n in range(WIDE)]
    sines = [math.sin(2.0 * math.pi * n / WIDE) for n in range(WIDE)]
    row = np.arange(WIDE)
    product = row[:, None] * row[None, :] % WIDE
    dft[0, :, :WIDE] = np.array(cosines)[product]
    dft[0, :, WIDE:] = -np.array(sines)[product]
    vectors = np.zeros((3, RES, WIDE), np.float64)
    for r in range(RES):
        for m in range(WIDE):
            turn = 2.0 * math.pi * (r * m) / PERIOD
            vectors[0, r, m], vectors[1, r, m] = math.cos(turn), math.sin(turn)
            freq = r + BLOCKS * m
            signed = freq if freq < PERIOD // 2 else freq - PERIOD
            if freq != PERIOD // 2:
                vectors[2, r, m] = 2.0 * math.pi * signed / PERIOD / PERIOD
    return split_parts(dft)[0], vectors.astype(np.float32)


def turned(value, turn):
    real, imag = value
    turn = turn % 1.0
    if turn == 0.0:
        return real, imag
    if turn == 0.5:
        return -real, (None if imag is None else -imag)
    if turn == 0.75:
        return imag, -real
    if turn == 0.25:
        return (None if imag is None else -imag), real
    cosine, sine = math.cos(2.0 * math.pi * turn), math.sin(2.0 * math.pi * turn)
    if imag is None:
        return real * cosine, real * sine
    return real * cosine - imag * sine, real * sine + imag * cosine


def plus(a, b):
    if b is None:
        return a
    return b if a is None else a + b


def minus(a, b):
    if b is None:
        return a
    return -b if a is None else a - b


def real_dft(values):
    count = len(values)
    if count == 2:
        return [(values[0] + values[1], None), (values[0] - values[1], None)]
    even, odd = real_dft(values[0::2]), real_dft(values[1::2])
    half, quarter = count // 2, count // 4
    result = [None] * (half + 1)
    for k in range(quarter + 1):
        spun = turned(odd[k], -k / count)
        result[k] = (plus(even[k][0], spun[0]), plus(even[k][1], spun[1]))
        mirror = (minus(even[k][0], spun[0]), minus(spun[1], even[k][1]))
        if k < quarter:
            result[half - k] = mirror
    return result


def real_inverse(spectrum):
    count = 2 * (len(spectrum) - 1)
    half, quarter = count // 2, count // 4
    if count == 2:
        return [spectrum[0][0] + spectrum[1][0], spectrum[0][0] - spectrum[1][0]]
    evens, odds = [], []
    for r in range(quarter + 1):
        low, high = spectrum[r], spectrum[half - r]
        total = (plus(low[0], high[0]), minus(low[1], high[1]))
        differ = (minus(low[0], high[0]), plus(low[1], high[1]))
        evens.append(total)
        odds.append(turned(differ, r / count))
    result = [None] * count
    result[0::2] = real_inverse(evens)
    result[1::2] = real_inverse(odds)
    return result


def store_split(target, first, second, value):
    high = value.astype(jnp.bfloat16)
    target[first] = high
    target[second] = (value - high.astype(jnp.float32)).astype(jnp.bfloat16)


def wide_product(lines, matrix):
    half = lines.shape[0] // 2
    main = jnp.dot(lines[...], matrix[0], preferred_element_type=jnp.float32)
    rest = jnp.dot(lines[:half], matrix[1], preferred_element_type=jnp.float32)
    both = main[:half] + main[half:] + rest
    quarter = half // 2
    return both[:quarter, :WIDE], both[:quarter, WIDE:], both[quarter:, :WIDE], both[quarter:, WIDE:]


def residue_part(some, residues, lines, matrix, vectors):
    def put(i, place, value):
        store_split(
            lines, pl.ds(96 * place + 32 * i, 32), pl.ds(192 + 96 * place + 32 * i, 32), value
        )

    for i, r in enumerate(some):
        cosine, sine = vectors[0, r : r + 1], vectors[1, r : r + 1]
        real, imag = residues[r, 0], residues[r, 1]
        put(i, 0, real * cosine + imag * sine)
        put(i, 1, imag * cosine - real * sine)
    rc, rs, ic, is_ = wide_product(lines, matrix)
    real, imag = rc - is_, rs + ic
    for i, r in enumerate(some):
        wave, at = vectors[2, r : r + 1], slice(32 * i, 32 * i + 32)
        put(i, 0, -wave * imag[at])
        put(i, 1, wave * real[at])
    rc, rs, ic, is_ = wide_product(lines, matrix)
    real, imag = rc + is_, ic - rs
    for i, r in enumerate(some):
        cosine, sine = vectors[0, r : r + 1], vectors[1, r : r + 1]
        at = slice(32 * i, 32 * i + 32)
        residues[r, 0] = real[at] * cosine - imag[at] * sine
        residues[r, 1] = real[at] * sine + imag[at] * cosine


def x_lines_kernel(lines_ref, after_ref, matrix, vectors, out_ref, work, residues, lines, sent):
    parts = [(pl.ds(16 * g, 16), pl.ds(128 * h, 128)) for g in range(2) for h in range(2)]
    outgoing = []
    for i, (rows, lanes) in enumerate(parts):
        here = (slice(None), rows, lanes)
        outgoing.append(pltpu.make_async_copy(work.at[here], out_ref.at[here], sent.at[i]))
        for r, (real, imag) in enumerate(real_dft([lines_ref[PLACE[p], rows, lanes] for p in range(BLOCKS)])):
            residues[r, 0, rows, lanes] = real
            residues[r, 1, rows, lanes] = jnp.zeros_like(real) if imag is None else imag
    for first in range(0, RES, 3):
        residue_part(range(first, first + 3), residues, lines, matrix, vectors)
    for copy, (rows, lanes) in zip(outgoing, parts):
        spectrum = []
        for r in range(RES):
            imag = None if r in (0, RES - 1) else residues[r, 1, rows, lanes]
            spectrum.append((residues[r, 0, rows, lanes], imag))
        for p, value in enumerate(real_inverse(spectrum)):
            work[PLACE[p], rows, lanes] = value
        copy.start()
    for copy in outgoing:
        copy.wait()


@functools.lru_cache(maxsize=None)
def ring_matrices():
    blocks = circulant_blocks()
    parts = np.zeros((16, WIDE, 4 * WIDE), np.float64)
    for own in range(4):
        for core in range(2):
            rows = slice(128 * core, 128 * core + 128)
            order = np.concatenate([np.arange(128) + 128 * core, np.arange(128) + 128 * (1 - core)])
            for k in range(4):
                target = parts[4 * own + 2 * core + k // 2, 128 * (k % 2) : 128 * (k % 2) + 128]
                for d in range(4):
                    block = blocks[(4 * d + own - (own - k) % 4) % BLOCKS][rows][:, order] / 4.0
                    target[:, :WIDE] += block
                    target[:, WIDE : 2 * WIDE] += block * (1 - 2 * (d % 2))
                    target[:, 2 * WIDE : 3 * WIDE] += 2.0 * block * (1, 0, -1, 0)[d]
                    target[:, 3 * WIDE :] -= 2.0 * block * (0, 1, 0, -1)[d]
    return split_parts(parts)


def load_kernel(me_ref, after_ref, matrix_ref, matrix, arrived):
    first = 2 * (me_ref[0] & 7)
    copy = pltpu.make_async_copy(matrix_ref.at[pl.ds(first, 2)], matrix, arrived)
    copy.start()
    copy.wait()


def ring_terms(pair, pieces, matrix, lines):
    for half, piece in enumerate(pieces):
        lanes = pl.ds(128 * half, 128)
        for group in range(16):
            at = pl.ds(16 * group, 16)
            w0, w1, w2, w3 = (piece[i, at, :] for i in (0, 3, 2, 1))
            values = (w0 + w2 + (w1 + w3), w0 + w2 - (w1 + w3), w0 - w2, w3 - w1)
            for value, offset, gap in zip(values, (0, 512, 1024, 1280), (256, 256, 512, 512)):
                store_split(
                    lines, (pl.ds(offset + 16 * group, 16), lanes), (pl.ds(offset + gap + 16 * group, 16), lanes), value
                )

    def product(offset, count, columns):
        main = jnp.dot(
            lines[offset : offset + 2 * count, :], matrix[pair, 0, :, columns], preferred_element_type=jnp.float32
        )
        rest = jnp.dot(
            lines[offset : offset + count, :], matrix[pair, 1, :, columns], preferred_element_type=jnp.float32
        )
        return main[:count] + main[count:] + rest

    both = product(1024, 512, slice(2 * WIDE, 4 * WIDE))
    return (
        product(0, 256, slice(0, WIDE)),
        product(512, 256, slice(WIDE, 2 * WIDE)),
        both[:256, :WIDE] - both[256:, WIDE:],
        both[:256, WIDE:] + both[256:, :WIDE],
    )


def y_first_kernel(p2, p3, matrix, sums, lines):
    for i, term in enumerate(ring_terms(1, (p2, p3), matrix, lines)):
        sums[i] = term


def y_lines_kernel(p0, p1, matrix, sums, own_ref, sent_ref, lines):
    z0, z2, real, imag = (sums[i] + term for i, term in enumerate(ring_terms(0, (p0, p1), matrix, lines)))
    for j, value in enumerate((z0 + z2 + real, z0 - z2 - imag, z0 + z2 - real, z0 - z2 + imag)):
        own_ref[j] = value[:, :128]
        sent_ref[j] = value[:, 128:]


def add_kernel(own_ref, other_ref, *out_refs):
    for j, out_ref in enumerate(out_refs):
        out_ref[...] = own_ref[j] + other_ref[j]


def whole(shape):
    return pl.BlockSpec(shape, lambda *_: (0,) * len(shape))


def any_place():
    return pl.BlockSpec(memory_space=pl.ANY)


def in_hbm():
    return pl.BlockSpec(memory_space=pltpu.HBM)


def in_vmem():
    return pl.BlockSpec(memory_space=pltpu.VMEM)


def in_smem():
    return pl.BlockSpec(memory_space=pltpu.SMEM)


def x_lines(lines, after):
    matrix, vectors = residue_tables()
    return pl.pallas_call(
        x_lines_kernel,
        in_specs=[in_vmem(), any_place(), in_vmem(), in_vmem()],
        out_specs=any_place(),
        out_shape=jax.ShapeDtypeStruct((BLOCKS, 32, WIDE), jnp.float32),
        scratch_shapes=[
            pltpu.VMEM((BLOCKS, 32, WIDE), jnp.float32),
            pltpu.VMEM((RES, 2, 32, WIDE), jnp.float32),
            pltpu.VMEM((384, WIDE), jnp.bfloat16),
            pltpu.SemaphoreType.DMA((4,)),
        ],
        cost_estimate=pl.CostEstimate(flops=900_000_000, bytes_accessed=1_000_000, transcendentals=0),
        compiler_params=pltpu.CompilerParams(vmem_limit_bytes=VMEM_LIMIT),
        name="x_lines",
    )(lines, after, jnp.asarray(matrix), jnp.asarray(vectors))


def load(me, after):
    matrices = ring_matrices()
    return pl.pallas_call(
        load_kernel,
        in_specs=[in_smem(), any_place(), in_hbm()],
        out_specs=in_vmem(),
        out_shape=jax.ShapeDtypeStruct((2,) + matrices.shape[1:], jnp.bfloat16),
        scratch_shapes=[pltpu.SemaphoreType.DMA],
        cost_estimate=pl.CostEstimate(flops=0, bytes_accessed=2_000_000, transcendentals=0),
        compiler_params=pltpu.CompilerParams(vmem_limit_bytes=VMEM_MOST),
        name="load",
    )(me, after, jnp.asarray(matrices))


def y_first(pieces, matrices):
    return pl.pallas_call(
        y_first_kernel,
        in_specs=[in_vmem()] * 3,
        out_specs=in_vmem(),
        out_shape=jax.ShapeDtypeStruct((4, 256, WIDE), jnp.float32),
        scratch_shapes=[pltpu.VMEM((2048, WIDE), jnp.bfloat16)],
        cost_estimate=pl.CostEstimate(flops=1_000_000_000, bytes_accessed=3_000_000, transcendentals=0),
        compiler_params=pltpu.CompilerParams(vmem_limit_bytes=VMEM_LIMIT),
        name="y_first",
    )(*pieces, matrices)


def y_lines(pieces, matrices, sums):
    half = jax.ShapeDtypeStruct((4, 256, 128), jnp.float32)
    return pl.pallas_call(
        y_lines_kernel,
        in_specs=[in_vmem()] * 4,
        out_specs=[in_vmem()] * 2,
        out_shape=[half] * 2,
        scratch_shapes=[pltpu.VMEM((2048, WIDE), jnp.bfloat16)],
        cost_estimate=pl.CostEstimate(flops=100_000_000_000, bytes_accessed=4_000_000, transcendentals=0),
        compiler_params=pltpu.CompilerParams(vmem_limit_bytes=VMEM_LIMIT),
        name="y_lines",
    )(*pieces, matrices, sums)


def add(own, other):
    return pl.pallas_call(
        add_kernel,
        in_specs=[in_vmem()] * 2,
        out_specs=[in_vmem()] * 4,
        out_shape=[jax.ShapeDtypeStruct((256, 128), jnp.float32)] * 4,
        cost_estimate=pl.CostEstimate(flops=200_000, bytes_accessed=1_500_000, transcendentals=0),
        compiler_params=pltpu.CompilerParams(vmem_limit_bytes=VMEM_LIMIT),
        name="add",
    )(own, other)


def pack_kernel(me_ref, fields, x_ref, q0, q1, q2, q3, lines, arrived):
    own_y = me_ref[0] >> 3
    copies = []
    for i in range(4):
        at = (slice(None), pl.ds(8 * i, 8))
        lines[at] = fields[i // 2 * 2, i % 2].T.reshape(16, 8, 256)
        copies.append(pltpu.make_async_copy(lines.at[at], x_ref.at[at], arrived.at[i]))
        copies[-1].start()
    for j, quarter in enumerate((q0, q1, q2, q3)):
        rows = pl.ds(pl.multiple_of(((own_y + j) & 3) * 64, 64), 64)
        for i in range(4):
            quarter[64 * i : 64 * i + 64, :] = fields[i // 2, i % 2, rows, :]
    for copy in copies:
        copy.wait()


def pack(me, fields):
    quarter = jax.ShapeDtypeStruct((256, 128), jnp.float32)
    return pl.pallas_call(
        pack_kernel,
        in_specs=[in_smem(), in_vmem()],
        out_specs=[any_place()] + [in_vmem()] * 4,
        out_shape=[jax.ShapeDtypeStruct((16, 32, 256), jnp.float32)] + [quarter] * 4,
        scratch_shapes=[pltpu.VMEM((16, 32, 256), jnp.float32), pltpu.SemaphoreType.DMA((4,))],
        cost_estimate=pl.CostEstimate(flops=0, bytes_accessed=2_000_000, transcendentals=0),
        compiler_params=pltpu.CompilerParams(vmem_limit_bytes=VMEM_LIMIT),
        name="pack",
    )(me, fields)


def shifted(value, axis, distance):
    pairs = []
    for i in range(32):
        at = [i // 8, i // 2 % 4, i % 2]
        at[axis] = (at[axis] + distance) % 4
        pairs.append((i, at[0] * 8 + at[1] * 2 + at[2]))
    return lax.ppermute(value, "gy", pairs)


def other_core(value):
    return lax.ppermute(value, "gy", [(i, i ^ 1) for i in range(32)])


def ring_swap(quarters):
    moved = {j: shifted(quarters[j], 0, j) for j in (1, 3, 2)}
    return [quarters[0]] + [moved[j] for j in (1, 2, 3)]


def ring_gather(held):
    moved = {j: shifted(held, 1, j) for j in (1, 3, 2)}
    return [held] + [moved[j] for j in (1, 2, 3)]


def base_kernel(
    fields_ref, poles_ref, stretch_ref, eps_ref, rates_ref, x_prof, y_prof, after_ref,
    next_poles, base, scale, vectors, fields, poles, stretch, inverse_eps, rates, out, arrived, sent
):
    pairs = [(poles_ref, poles), (rates_ref, rates), (fields_ref, fields), (eps_ref, inverse_eps), (stretch_ref, stretch)]
    copies = [pltpu.make_async_copy(a, b, arrived.at[k]) for k, (a, b) in enumerate(pairs)]
    for copy in copies:
        copy.start()
    conduct_x, stretch_x, shift_x = x_prof[0:1, :], x_prof[1:2, :], x_prof[2:3, :]
    conduct_y, stretch_y, shift_y = y_prof[0:1, :], y_prof[1:2, :], y_prof[2:3, :]
    decay_y = conduct_y / stretch_y + shift_y

    def down(row):
        return jnp.broadcast_to(row, (128, 256)).T

    decay_x = down(conduct_x / stretch_x + shift_x)
    vectors[0:1, :] = 1.0 / stretch_x
    vectors[1:2, :] = section_step * conduct_x / (stretch_x * stretch_x)
    vectors[2:3, 0:128] = 1.0 / stretch_y
    vectors[3:4, 0:128] = section_step * conduct_y / (stretch_y * stretch_y)
    for copy in copies[:3]:
        copy.wait()
    for plane in range(2):
        polar, current, ez = poles[0, plane], poles[1, plane], fields[0, plane]
        damping, resonance, plasma = (rates[i].astype(jnp.float32) for i in range(3))
        out[0, plane] = polar + section_step * current
        out[1, plane] = current + section_step * (plasma * ez - damping * current - resonance * polar)
    result = pltpu.make_async_copy(out, next_poles, sent)
    result.start()
    for copy in copies[3:]:
        copy.wait()
    eps = section_step * inverse_eps[...]
    scale[...] = eps
    for plane in range(2):
        s0, s1, s2, s3 = (stretch[i, plane] for i in range(4))
        base[0, plane] = fields[0, plane] + eps * (s1 - s3 - poles[1, plane])
        base[1, plane] = fields[1, plane] - section_step * s2
        base[2, plane] = fields[2, plane] + section_step * s0
        base[3, plane] = s0 - section_step * (decay_x * s0)
        base[4, plane] = s1 - section_step * (decay_x * s1)
        base[5, plane] = s2 - section_step * (decay_y * s2)
        base[6, plane] = s3 - section_step * (decay_y * s3)
    result.wait()


def base_part(fields, pole_state, stretch_state, inverse_permittivity, pole_rates, x_profile, y_profile, after):
    return pl.pallas_call(
        base_kernel,
        in_specs=[any_place()] * 5 + [in_vmem()] * 2 + [any_place()],
        out_specs=[in_hbm(), in_vmem(), in_vmem(), in_vmem()],
        out_shape=[
            jax.ShapeDtypeStruct((2, 2, 256, 128), jnp.float32),
            jax.ShapeDtypeStruct((7, 2, 256, 128), jnp.float32),
            jax.ShapeDtypeStruct((256, 128), jnp.float32),
            jax.ShapeDtypeStruct((8, 256), jnp.float32),
        ],
        scratch_shapes=[
            pltpu.VMEM((3, 2, 256, 128), jnp.float32),
            pltpu.VMEM((2, 2, 256, 128), jnp.float32),
            pltpu.VMEM((4, 2, 256, 128), jnp.float32),
            pltpu.VMEM((256, 128), jnp.float32),
            pltpu.VMEM((3, 256, 128), jnp.bfloat16),
            pltpu.VMEM((2, 2, 256, 128), jnp.float32),
            pltpu.SemaphoreType.DMA((5,)),
            pltpu.SemaphoreType.DMA,
        ],
        cost_estimate=pl.CostEstimate(flops=3_000_000, bytes_accessed=5_000_000, transcendentals=0),
        compiler_params=pltpu.CompilerParams(vmem_limit_bytes=VMEM_LIMIT),
        name="base",
    )(fields, pole_state, stretch_state, inverse_permittivity, pole_rates, x_profile, y_profile, after)


def finish_kernel(
    me_ref, base, scale, vectors, x_deriv, q0, q1, q2, q3, next_fields, next_stretch, y_deriv, fields, stretch, sent
):
    own_y = me_ref[0] >> 3
    for j, quarter in enumerate((q0, q1, q2, q3)):
        rows = pl.ds(pl.multiple_of(((own_y - j) & 3) * 64, 64), 64)
        for i in range(4):
            y_deriv[i, rows, :] = quarter[64 * i : 64 * i + 64, :]
    over_y, feed_y = vectors[2:3, 0:128], vectors[3:4, 0:128]
    over_x, feed_x = (jnp.broadcast_to(vectors[i : i + 1, :], (128, 256)).T for i in range(2))
    eps = scale[...]
    copies = []

    def send(source, target):
        copy = pltpu.make_async_copy(source, target, sent.at[len(copies)])
        copy.start()
        copies.append(copy)

    for plane in range(2):
        ez_dy, hx_dy = y_deriv[plane], y_deriv[2 + plane]
        stretch[2, plane] = base[5, plane] - feed_y * ez_dy
        stretch[3, plane] = base[6, plane] - feed_y * hx_dy
        fields[1, plane] = base[1, plane] - section_step * (over_y * ez_dy)
        send(stretch.at[pl.ds(2, 2), plane], next_stretch.at[pl.ds(2, 2), plane])
        send(fields.at[1, plane], next_fields.at[1, plane])
    for plane in range(2):
        ez_dx = x_deriv[:, 8 * plane : 8 * plane + 8, :].reshape(128, 256).T
        hy_dx = x_deriv[:, 16 + 8 * plane : 24 + 8 * plane, :].reshape(128, 256).T
        stretch[0, plane] = base[3, plane] - feed_x * ez_dx
        stretch[1, plane] = base[4, plane] - feed_x * hy_dx
        fields[2, plane] = base[2, plane] + section_step * (over_x * ez_dx)
        fields[0, plane] = base[0, plane] + eps * (over_x * hy_dx - over_y * y_deriv[2 + plane])
        send(stretch.at[pl.ds(0, 2), plane], next_stretch.at[pl.ds(0, 2), plane])
        send(fields.at[2, plane], next_fields.at[2, plane])
        send(fields.at[0, plane], next_fields.at[0, plane])
    for copy in copies:
        copy.wait()


def finish(me, base, scale, vectors, x_deriv, quarters):
    return pl.pallas_call(
        finish_kernel,
        in_specs=[in_smem()] + [in_vmem()] * 8,
        out_specs=[in_hbm()] * 2,
        out_shape=[jax.ShapeDtypeStruct((count, 2, 256, 128), jnp.float32) for count in (3, 4)],
        scratch_shapes=[
            pltpu.VMEM((4, 256, 128), jnp.float32),
            pltpu.VMEM((3, 2, 256, 128), jnp.float32),
            pltpu.VMEM((4, 2, 256, 128), jnp.float32),
            pltpu.SemaphoreType.DMA((10,)),
        ],
        cost_estimate=pl.CostEstimate(flops=3_000_000, bytes_accessed=5_000_000, transcendentals=0),
        compiler_params=pltpu.CompilerParams(vmem_limit_bytes=VMEM_LIMIT),
        name="finish",
    )(me, base, scale, vectors, x_deriv, *quarters)


def swap_x(lines):
    return lax.all_to_all(lines, "gx", split_axis=0, concat_axis=0, tiled=True, axis_index_groups=[list(RING)])


def shards(fields, pole_state, stretch_state, inverse_permittivity, pole_rates, x_profile, y_profile):
    me = lax.axis_index("gy").astype(jnp.int32).reshape(1)
    x_packed, *y_packed = pack(me, fields)
    x_sorted = swap_x(x_packed)
    y_held = jnp.stack(ring_swap(y_packed))
    y_pieces = ring_gather(y_held)
    x_lined = x_lines(x_sorted, y_held)
    x_deriv = swap_x(x_lined)
    matrices = load(me, x_lined)
    own, sent = y_lines(y_pieces[:2], matrices, y_first(y_pieces[2:], matrices))
    y_lined = add(own, other_core(sent))
    next_poles, base, scale, vectors = base_part(
        fields, pole_state, stretch_state, inverse_permittivity, pole_rates, x_profile, y_profile, y_lined[0]
    )
    next_fields, next_stretch = finish(me, base, scale, vectors, x_deriv, ring_swap(y_lined))
    return next_fields, next_poles, next_stretch


def solution(mesh):
    return jax.shard_map(
        shards,
        mesh=mesh,
        in_specs=(
            P(None, None, "gx", "gy"),
            P(None, None, "gx", "gy"),
            P(None, None, "gx", "gy"),
            P("gx", "gy"),
            P(None, "gx", "gy"),
            P(None, "gx"),
            P(None, "gy"),
        ),
        out_specs=(P(None, None, "gx", "gy"), P(None, None, "gx", "gy"), P(None, None, "gx", "gy")),
        check_vma=False,
    )
```

```python
import functools
import math

import jax
import jax.numpy as jnp
import ml_dtypes
import numpy as np
from jax import lax
from jax.experimental import pallas as pl
from jax.experimental.pallas import tpu as pltpu
from jax.sharding import PartitionSpec as P

section_step = 0.25
PERIOD = 4096
BLOCKS = 16
WIDE = PERIOD // BLOCKS
RES = BLOCKS // 2 + 1
RING = (12, 13, 14, 15, 11, 10, 9, 8, 4, 5, 6, 7, 3, 2, 1, 0)
PLACE = tuple(RING.index(p) for p in range(BLOCKS))
VMEM_LIMIT = 16 * 1024 * 1024
VMEM_MOST = 49 * 1024 * 1024


@functools.lru_cache(maxsize=None)
def circulant_blocks():
    table = np.zeros(PERIOD, np.float64)
    for n in range(1, PERIOD):
        if n != PERIOD // 2:
            sign = -1.0 if n % 2 else 1.0
            table[n] = math.pi / PERIOD * sign / math.tan(math.pi * n / PERIOD)
    row = np.arange(WIDE)
    offset = row[None, :] - row[:, None]
    return [table[(WIDE * d + offset) % PERIOD] for d in range(BLOCKS)]


def split_parts(parts):
    high = parts.astype(np.float32).astype(ml_dtypes.bfloat16)
    low = (parts - high.astype(np.float64)).astype(np.float32).astype(ml_dtypes.bfloat16)
    return np.stack([high, low], 1)


@functools.lru_cache(maxsize=None)
def residue_tables():
    dft = np.zeros((1, WIDE, 2 * WIDE), np.float64)
    cosines = [math.cos(2.0 * math.pi * n / WIDE) for n in range(WIDE)]
    sines = [math.sin(2.0 * math.pi * n / WIDE) for n in range(WIDE)]
    row = np.arange(WIDE)
    product = row[:, None] * row[None, :] % WIDE
    dft[0, :, :WIDE] = np.array(cosines)[product]
    dft[0, :, WIDE:] = -np.array(sines)[product]
    vectors = np.zeros((3, RES, WIDE), np.float64)
    for r in range(RES):
        for m in range(WIDE):
            turn = 2.0 * math.pi * (r * m) / PERIOD
            vectors[0, r, m], vectors[1, r, m] = math.cos(turn), math.sin(turn)
            freq = r + BLOCKS * m
            signed = freq if freq < PERIOD // 2 else freq - PERIOD
            if freq != PERIOD // 2:
                vectors[2, r, m] = 2.0 * math.pi * signed / PERIOD / PERIOD
    return split_parts(dft)[0], vectors.astype(np.float32)


def turned(value, turn):
    real, imag = value
    turn = turn % 1.0
    if turn == 0.0:
        return real, imag
    if turn == 0.5:
        return -real, (None if imag is None else -imag)
    if turn == 0.75:
        return imag, -real
    if turn == 0.25:
        return (None if imag is None else -imag), real
    cosine, sine = math.cos(2.0 * math.pi * turn), math.sin(2.0 * math.pi * turn)
    if imag is None:
        return real * cosine, real * sine
    return real * cosine - imag * sine, real * sine + imag * cosine


def plus(a, b):
    if b is None:
        return a
    return b if a is None else a + b


def minus(a, b):
    if b is None:
        return a
    return -b if a is None else a - b


def real_dft(values):
    count = len(values)
    if count == 2:
        return [(values[0] + values[1], None), (values[0] - values[1], None)]
    even, odd = real_dft(values[0::2]), real_dft(values[1::2])
    half, quarter = count // 2, count // 4
    result = [None] * (half + 1)
    for k in range(quarter + 1):
        spun = turned(odd[k], -k / count)
        result[k] = (plus(even[k][0], spun[0]), plus(even[k][1], spun[1]))
        mirror = (minus(even[k][0], spun[0]), minus(spun[1], even[k][1]))
        if k < quarter:
            result[half - k] = mirror
    return result


def real_inverse(spectrum):
    count = 2 * (len(spectrum) - 1)
    half, quarter = count // 2, count // 4
    if count == 2:
        return [spectrum[0][0] + spectrum[1][0], spectrum[0][0] - spectrum[1][0]]
    evens, odds = [], []
    for r in range(quarter + 1):
        low, high = spectrum[r], spectrum[half - r]
        total = (plus(low[0], high[0]), minus(low[1], high[1]))
        differ = (minus(low[0], high[0]), plus(low[1], high[1]))
        evens.append(total)
        odds.append(turned(differ, r / count))
    result = [None] * count
    result[0::2] = real_inverse(evens)
    result[1::2] = real_inverse(odds)
    return result


def store_split(target, first, second, value):
    high = value.astype(jnp.bfloat16)
    target[first] = high
    target[second] = (value - high.astype(jnp.float32)).astype(jnp.bfloat16)


def wide_product(lines, matrix):
    half = lines.shape[0] // 2
    main = jnp.dot(lines[...], matrix[0], preferred_element_type=jnp.float32)
    rest = jnp.dot(lines[:half], matrix[1], preferred_element_type=jnp.float32)
    both = main[:half] + main[half:] + rest
    quarter = half // 2
    return both[:quarter, :WIDE], both[:quarter, WIDE:], both[quarter:, :WIDE], both[quarter:, WIDE:]


def residue_part(some, residues, lines, matrix, vectors):
    def put(i, place, value):
        store_split(
            lines, pl.ds(96 * place + 32 * i, 32), pl.ds(192 + 96 * place + 32 * i, 32), value
        )

    for i, r in enumerate(some):
        cosine, sine = vectors[0, r : r + 1], vectors[1, r : r + 1]
        real, imag = residues[r, 0], residues[r, 1]
        put(i, 0, real * cosine + imag * sine)
        put(i, 1, imag * cosine - real * sine)
    rc, rs, ic, is_ = wide_product(lines, matrix)
    real, imag = rc - is_, rs + ic
    for i, r in enumerate(some):
        wave, at = vectors[2, r : r + 1], slice(32 * i, 32 * i + 32)
        put(i, 0, -wave * imag[at])
        put(i, 1, wave * real[at])
    rc, rs, ic, is_ = wide_product(lines, matrix)
    real, imag = rc + is_, ic - rs
    for i, r in enumerate(some):
        cosine, sine = vectors[0, r : r + 1], vectors[1, r : r + 1]
        at = slice(32 * i, 32 * i + 32)
        residues[r, 0] = real[at] * cosine - imag[at] * sine
        residues[r, 1] = real[at] * sine + imag[at] * cosine


def x_lines_kernel(lines_ref, after_ref, matrix, vectors, out_ref, work, residues, lines, sent):
    parts = [(pl.ds(16 * g, 16), pl.ds(128 * h, 128)) for g in range(2) for h in range(2)]
    outgoing = []
    for i, (rows, lanes) in enumerate(parts):
        here = (slice(None), rows, lanes)
        outgoing.append(pltpu.make_async_copy(work.at[here], out_ref.at[here], sent.at[i]))
        for r, (real, imag) in enumerate(real_dft([lines_ref[PLACE[p], rows, lanes] for p in range(BLOCKS)])):
            residues[r, 0, rows, lanes] = real
            residues[r, 1, rows, lanes] = jnp.zeros_like(real) if imag is None else imag
    for first in range(0, RES, 3):
        residue_part(range(first, first + 3), residues, lines, matrix, vectors)
    for copy, (rows, lanes) in zip(outgoing, parts):
        spectrum = []
        for r in range(RES):
            imag = None if r in (0, RES - 1) else residues[r, 1, rows, lanes]
            spectrum.append((residues[r, 0, rows, lanes], imag))
        for p, value in enumerate(real_inverse(spectrum)):
            work[PLACE[p], rows, lanes] = value
        copy.start()
    for copy in outgoing:
        copy.wait()


@functools.lru_cache(maxsize=None)
def ring_matrices():
    blocks = circulant_blocks()
    parts = np.zeros((16, WIDE, 4 * WIDE), np.float64)
    for own in range(4):
        for core in range(2):
            rows = slice(128 * core, 128 * core + 128)
            order = np.concatenate([np.arange(128) + 128 * core, np.arange(128) + 128 * (1 - core)])
            for k in range(4):
                target = parts[4 * own + 2 * core + k // 2, 128 * (k % 2) : 128 * (k % 2) + 128]
                for d in range(4):
                    block = blocks[(4 * d + own - (own - k) % 4) % BLOCKS][rows][:, order] / 4.0
                    target[:, :WIDE] += block
                    target[:, WIDE : 2 * WIDE] += block * (1 - 2 * (d % 2))
                    target[:, 2 * WIDE : 3 * WIDE] += 2.0 * block * (1, 0, -1, 0)[d]
                    target[:, 3 * WIDE :] -= 2.0 * block * (0, 1, 0, -1)[d]
    return split_parts(parts)


def load_kernel(me_ref, after_ref, matrix_ref, matrix, arrived):
    first = 2 * (me_ref[0] & 7)
    copy = pltpu.make_async_copy(matrix_ref.at[pl.ds(first, 2)], matrix, arrived)
    copy.start()
    copy.wait()


def ring_terms(pair, pieces, matrix, lines):
    for half, piece in enumerate(pieces):
        lanes = pl.ds(128 * half, 128)
        for group in range(16):
            at = pl.ds(16 * group, 16)
            w0, w1, w2, w3 = (piece[i, at, :] for i in (0, 3, 2, 1))
            values = (w0 + w2 + (w1 + w3), w0 + w2 - (w1 + w3), w0 - w2, w3 - w1)
            for value, offset, gap in zip(values, (0, 512, 1024, 1280), (256, 256, 512, 512)):
                store_split(
                    lines, (pl.ds(offset + 16 * group, 16), lanes), (pl.ds(offset + gap + 16 * group, 16), lanes), value
                )

    def product(offset, count, columns):
        main = jnp.dot(
            lines[offset : offset + 2 * count, :], matrix[pair, 0, :, columns], preferred_element_type=jnp.float32
        )
        rest = jnp.dot(
            lines[offset : offset + count, :], matrix[pair, 1, :, columns], preferred_element_type=jnp.float32
        )
        return main[:count] + main[count:] + rest

    both = product(1024, 512, slice(2 * WIDE, 4 * WIDE))
    return (
        product(0, 256, slice(0, WIDE)),
        product(512, 256, slice(WIDE, 2 * WIDE)),
        both[:256, :WIDE] - both[256:, WIDE:],
        both[:256, WIDE:] + both[256:, :WIDE],
    )


def y_first_kernel(p2, p3, matrix, sums, lines):
    for i, term in enumerate(ring_terms(1, (p2, p3), matrix, lines)):
        sums[i] = term


def y_lines_kernel(p0, p1, matrix, sums, own_ref, sent_ref, lines):
    z0, z2, real, imag = (sums[i] + term for i, term in enumerate(ring_terms(0, (p0, p1), matrix, lines)))
    for j, value in enumerate((z0 + z2 + real, z0 - z2 - imag, z0 + z2 - real, z0 - z2 + imag)):
        own_ref[j] = value[:, :128]
        sent_ref[j] = value[:, 128:]


def add_kernel(own_ref, other_ref, *out_refs):
    for j, out_ref in enumerate(out_refs):
        out_ref[...] = own_ref[j] + other_ref[j]


def whole(shape):
    return pl.BlockSpec(shape, lambda *_: (0,) * len(shape))


def any_place():
    return pl.BlockSpec(memory_space=pl.ANY)


def in_hbm():
    return pl.BlockSpec(memory_space=pltpu.HBM)


def in_vmem():
    return pl.BlockSpec(memory_space=pltpu.VMEM)


def in_smem():
    return pl.BlockSpec(memory_space=pltpu.SMEM)


def x_lines(lines, after):
    matrix, vectors = residue_tables()
    return pl.pallas_call(
        x_lines_kernel,
        in_specs=[in_vmem(), any_place(), in_vmem(), in_vmem()],
        out_specs=any_place(),
        out_shape=jax.ShapeDtypeStruct((BLOCKS, 32, WIDE), jnp.float32),
        scratch_shapes=[
            pltpu.VMEM((BLOCKS, 32, WIDE), jnp.float32),
            pltpu.VMEM((RES, 2, 32, WIDE), jnp.float32),
            pltpu.VMEM((384, WIDE), jnp.bfloat16),
            pltpu.SemaphoreType.DMA((4,)),
        ],
        cost_estimate=pl.CostEstimate(flops=900_000_000, bytes_accessed=1_000_000, transcendentals=0),
        compiler_params=pltpu.CompilerParams(vmem_limit_bytes=VMEM_LIMIT),
        name="x_lines",
    )(lines, after, jnp.asarray(matrix), jnp.asarray(vectors))


def load(me, after):
    matrices = ring_matrices()
    return pl.pallas_call(
        load_kernel,
        in_specs=[in_smem(), any_place(), in_hbm()],
        out_specs=in_vmem(),
        out_shape=jax.ShapeDtypeStruct((2,) + matrices.shape[1:], jnp.bfloat16),
        scratch_shapes=[pltpu.SemaphoreType.DMA],
        cost_estimate=pl.CostEstimate(flops=0, bytes_accessed=2_000_000, transcendentals=0),
        compiler_params=pltpu.CompilerParams(vmem_limit_bytes=VMEM_MOST),
        name="load",
    )(me, after, jnp.asarray(matrices))


def y_first(pieces, matrices):
    return pl.pallas_call(
        y_first_kernel,
        in_specs=[in_vmem()] * 3,
        out_specs=in_vmem(),
        out_shape=jax.ShapeDtypeStruct((4, 256, WIDE), jnp.float32),
        scratch_shapes=[pltpu.VMEM((2048, WIDE), jnp.bfloat16)],
        cost_estimate=pl.CostEstimate(flops=1_000_000_000, bytes_accessed=3_000_000, transcendentals=0),
        compiler_params=pltpu.CompilerParams(vmem_limit_bytes=VMEM_LIMIT),
        name="y_first",
    )(*pieces, matrices)


def y_lines(pieces, matrices, sums):
    half = jax.ShapeDtypeStruct((4, 256, 128), jnp.float32)
    return pl.pallas_call(
        y_lines_kernel,
        in_specs=[in_vmem()] * 4,
        out_specs=[in_vmem()] * 2,
        out_shape=[half] * 2,
        scratch_shapes=[pltpu.VMEM((2048, WIDE), jnp.bfloat16)],
        cost_estimate=pl.CostEstimate(flops=100_000_000_000, bytes_accessed=4_000_000, transcendentals=0),
        compiler_params=pltpu.CompilerParams(vmem_limit_bytes=VMEM_LIMIT),
        name="y_lines",
    )(*pieces, matrices, sums)


def add(own, other):
    return pl.pallas_call(
        add_kernel,
        in_specs=[in_vmem()] * 2,
        out_specs=[in_vmem()] * 4,
        out_shape=[jax.ShapeDtypeStruct((256, 128), jnp.float32)] * 4,
        cost_estimate=pl.CostEstimate(flops=200_000, bytes_accessed=1_500_000, transcendentals=0),
        compiler_params=pltpu.CompilerParams(vmem_limit_bytes=VMEM_LIMIT),
        name="add",
    )(own, other)


def pack_kernel(me_ref, fields, x_ref, q0, q1, q2, q3, lines, arrived):
    own_y = me_ref[0] >> 3
    copies = []
    for i in range(4):
        at = (slice(None), pl.ds(8 * i, 8))
        lines[at] = fields[i // 2 * 2, i % 2].T.reshape(16, 8, 256)
        copies.append(pltpu.make_async_copy(lines.at[at], x_ref.at[at], arrived.at[i]))
        copies[-1].start()
    for j, quarter in enumerate((q0, q1, q2, q3)):
        rows = pl.ds(pl.multiple_of(((own_y + j) & 3) * 64, 64), 64)
        for i in range(4):
            quarter[64 * i : 64 * i + 64, :] = fields[i // 2, i % 2, rows, :]
    for copy in copies:
        copy.wait()


def pack(me, fields):
    quarter = jax.ShapeDtypeStruct((256, 128), jnp.float32)
    return pl.pallas_call(
        pack_kernel,
        in_specs=[in_smem(), in_vmem()],
        out_specs=[any_place()] + [in_vmem()] * 4,
        out_shape=[jax.ShapeDtypeStruct((16, 32, 256), jnp.float32)] + [quarter] * 4,
        scratch_shapes=[pltpu.VMEM((16, 32, 256), jnp.float32), pltpu.SemaphoreType.DMA((4,))],
        cost_estimate=pl.CostEstimate(flops=0, bytes_accessed=2_000_000, transcendentals=0),
        compiler_params=pltpu.CompilerParams(vmem_limit_bytes=VMEM_LIMIT),
        name="pack",
    )(me, fields)


def shifted(value, axis, distance):
    pairs = []
    for i in range(32):
        at = [i // 8, i // 2 % 4, i % 2]
        at[axis] = (at[axis] + distance) % 4
        pairs.append((i, at[0] * 8 + at[1] * 2 + at[2]))
    return lax.ppermute(value, "gy", pairs)


def other_core(value):
    return lax.ppermute(value, "gy", [(i, i ^ 1) for i in range(32)])


def ring_swap(quarters):
    moved = {j: shifted(quarters[j], 0, j) for j in (1, 3, 2)}
    return [quarters[0]] + [moved[j] for j in (1, 2, 3)]


def ring_gather(held):
    moved = {j: shifted(held, 1, j) for j in (1, 3, 2)}
    return [held] + [moved[j] for j in (1, 2, 3)]


def base_kernel(
    fields_ref, poles_ref, stretch_ref, eps_ref, rates_ref, x_prof, y_prof, after_ref,
    next_poles, base, scale, vectors, fields, poles, stretch, inverse_eps, rates, out, arrived, sent
):
    pairs = [(poles_ref, poles), (rates_ref, rates), (fields_ref, fields), (eps_ref, inverse_eps), (stretch_ref, stretch)]
    copies = [pltpu.make_async_copy(a, b, arrived.at[k]) for k, (a, b) in enumerate(pairs)]
    for copy in copies:
        copy.start()
    conduct_x, stretch_x, shift_x = x_prof[0:1, :], x_prof[1:2, :], x_prof[2:3, :]
    conduct_y, stretch_y, shift_y = y_prof[0:1, :], y_prof[1:2, :], y_prof[2:3, :]
    decay_y = conduct_y / stretch_y + shift_y

    def down(row):
        return jnp.broadcast_to(row, (128, 256)).T

    decay_x = down(conduct_x / stretch_x + shift_x)
    vectors[0:1, :] = 1.0 / stretch_x
    vectors[1:2, :] = section_step * conduct_x / (stretch_x * stretch_x)
    vectors[2:3, 0:128] = 1.0 / stretch_y
    vectors[3:4, 0:128] = section_step * conduct_y / (stretch_y * stretch_y)
    for copy in copies[:3]:
        copy.wait()
    for plane in range(2):
        polar, current, ez = poles[0, plane], poles[1, plane], fields[0, plane]
        damping, resonance, plasma = (rates[i].astype(jnp.float32) for i in range(3))
        out[0, plane] = polar + section_step * current
        out[1, plane] = current + section_step * (plasma * ez - damping * current - resonance * polar)
    result = pltpu.make_async_copy(out, next_poles, sent)
    result.start()
    for copy in copies[3:]:
        copy.wait()
    eps = section_step * inverse_eps[...]
    scale[...] = eps
    for plane in range(2):
        s0, s1, s2, s3 = (stretch[i, plane] for i in range(4))
        base[0, plane] = fields[0, plane] + eps * (s1 - s3 - poles[1, plane])
        base[1, plane] = fields[1, plane] - section_step * s2
        base[2, plane] = fields[2, plane] + section_step * s0
        base[3, plane] = s0 - section_step * (decay_x * s0)
        base[4, plane] = s1 - section_step * (decay_x * s1)
        base[5, plane] = s2 - section_step * (decay_y * s2)
        base[6, plane] = s3 - section_step * (decay_y * s3)
    result.wait()


def base_part(fields, pole_state, stretch_state, inverse_permittivity, pole_rates, x_profile, y_profile, after):
    return pl.pallas_call(
        base_kernel,
        in_specs=[any_place()] * 5 + [in_vmem()] * 2 + [any_place()],
        out_specs=[in_hbm(), in_vmem(), in_vmem(), in_vmem()],
        out_shape=[
            jax.ShapeDtypeStruct((2, 2, 256, 128), jnp.float32),
            jax.ShapeDtypeStruct((7, 2, 256, 128), jnp.float32),
            jax.ShapeDtypeStruct((256, 128), jnp.float32),
            jax.ShapeDtypeStruct((8, 256), jnp.float32),
        ],
        scratch_shapes=[
            pltpu.VMEM((3, 2, 256, 128), jnp.float32),
            pltpu.VMEM((2, 2, 256, 128), jnp.float32),
            pltpu.VMEM((4, 2, 256, 128), jnp.float32),
            pltpu.VMEM((256, 128), jnp.float32),
            pltpu.VMEM((3, 256, 128), jnp.bfloat16),
            pltpu.VMEM((2, 2, 256, 128), jnp.float32),
            pltpu.SemaphoreType.DMA((5,)),
            pltpu.SemaphoreType.DMA,
        ],
        cost_estimate=pl.CostEstimate(flops=3_000_000, bytes_accessed=5_000_000, transcendentals=0),
        compiler_params=pltpu.CompilerParams(vmem_limit_bytes=VMEM_LIMIT),
        name="base",
    )(fields, pole_state, stretch_state, inverse_permittivity, pole_rates, x_profile, y_profile, after)


def finish_kernel(
    me_ref, base, scale, vectors, x_deriv, q0, q1, q2, q3, next_fields, next_stretch, y_deriv, fields, stretch, sent
):
    own_y = me_ref[0] >> 3
    for j, quarter in enumerate((q0, q1, q2, q3)):
        rows = pl.ds(pl.multiple_of(((own_y - j) & 3) * 64, 64), 64)
        for i in range(4):
            y_deriv[i, rows, :] = quarter[64 * i : 64 * i + 64, :]
    over_y, feed_y = vectors[2:3, 0:128], vectors[3:4, 0:128]
    over_x, feed_x = (jnp.broadcast_to(vectors[i : i + 1, :], (128, 256)).T for i in range(2))
    eps = scale[...]
    copies = []

    def send(source, target):
        copy = pltpu.make_async_copy(source, target, sent.at[len(copies)])
        copy.start()
        copies.append(copy)

    for plane in range(2):
        ez_dy, hx_dy = y_deriv[plane], y_deriv[2 + plane]
        stretch[2, plane] = base[5, plane] - feed_y * ez_dy
        stretch[3, plane] = base[6, plane] - feed_y * hx_dy
        fields[1, plane] = base[1, plane] - section_step * (over_y * ez_dy)
        send(stretch.at[pl.ds(2, 2), plane], next_stretch.at[pl.ds(2, 2), plane])
        send(fields.at[1, plane], next_fields.at[1, plane])
    for plane in range(2):
        ez_dx = x_deriv[:, 8 * plane : 8 * plane + 8, :].reshape(128, 256).T
        hy_dx = x_deriv[:, 16 + 8 * plane : 24 + 8 * plane, :].reshape(128, 256).T
        stretch[0, plane] = base[3, plane] - feed_x * ez_dx
        stretch[1, plane] = base[4, plane] - feed_x * hy_dx
        fields[2, plane] = base[2, plane] + section_step * (over_x * ez_dx)
        fields[0, plane] = base[0, plane] + eps * (over_x * hy_dx - over_y * y_deriv[2 + plane])
        send(stretch.at[pl.ds(0, 2), plane], next_stretch.at[pl.ds(0, 2), plane])
        send(fields.at[2, plane], next_fields.at[2, plane])
        send(fields.at[0, plane], next_fields.at[0, plane])
    for copy in copies:
        copy.wait()


def finish(me, base, scale, vectors, x_deriv, quarters):
    return pl.pallas_call(
        finish_kernel,
        in_specs=[in_smem()] + [in_vmem()] * 8,
        out_specs=[in_hbm()] * 2,
        out_shape=[jax.ShapeDtypeStruct((count, 2, 256, 128), jnp.float32) for count in (3, 4)],
        scratch_shapes=[
            pltpu.VMEM((4, 256, 128), jnp.float32),
            pltpu.VMEM((3, 2, 256, 128), jnp.float32),
            pltpu.VMEM((4, 2, 256, 128), jnp.float32),
            pltpu.SemaphoreType.DMA((10,)),
        ],
        cost_estimate=pl.CostEstimate(flops=3_000_000, bytes_accessed=5_000_000, transcendentals=0),
        compiler_params=pltpu.CompilerParams(vmem_limit_bytes=VMEM_LIMIT),
        name="finish",
    )(me, base, scale, vectors, x_deriv, *quarters)


def swap_x(lines):
    return lax.all_to_all(lines, "gx", split_axis=0, concat_axis=0, tiled=True, axis_index_groups=[list(RING)])


def shards(fields, pole_state, stretch_state, inverse_permittivity, pole_rates, x_profile, y_profile):
    me = lax.axis_index("gy").astype(jnp.int32).reshape(1)
    x_packed, *y_packed = pack(me, fields)
    x_sorted = swap_x(x_packed)
    y_held = jnp.stack(ring_swap(y_packed))
    y_pieces = ring_gather(y_held)
    x_lined = x_lines(x_sorted, y_held)
    x_deriv = swap_x(x_lined)
    matrices = load(me, x_lined)
    own, sent = y_lines(y_pieces[:2], matrices, y_first(y_pieces[2:], matrices))
    y_lined = add(own, other_core(sent))
    next_poles, base, scale, vectors = base_part(
        fields, pole_state, stretch_state, inverse_permittivity, pole_rates, x_profile, y_profile, y_lined[0]
    )
    next_fields, next_stretch = finish(me, base, scale, vectors, x_deriv, ring_swap(y_lined))
    return next_fields, next_poles, next_stretch


def solution(mesh):
    return jax.shard_map(
        shards,
        mesh=mesh,
        in_specs=(
            P(None, None, "gx", "gy"),
            P(None, None, "gx", "gy"),
            P(None, None, "gx", "gy"),
            P("gx", "gy"),
            P(None, "gx", "gy"),
            P(None, "gx"),
            P(None, "gy"),
        ),
        out_specs=(P(None, None, "gx", "gy"), P(None, None, "gx", "gy"), P(None, None, "gx", "gy")),
        check_vma=False,
    )
```

```python
import functools
import math

import jax
import jax.numpy as jnp
import ml_dtypes
import numpy as np
from jax import lax
from jax.experimental import pallas as pl
from jax.experimental.pallas import tpu as pltpu
from jax.sharding import PartitionSpec as P

section_step = 0.25
PERIOD = 4096
BLOCKS = 16
WIDE = PERIOD // BLOCKS
RES = BLOCKS // 2 + 1
RING = (12, 13, 14, 15, 11, 10, 9, 8, 4, 5, 6, 7, 3, 2, 1, 0)
PLACE = tuple(RING.index(p) for p in range(BLOCKS))
VMEM_LIMIT = 16 * 1024 * 1024
VMEM_MOST = 49 * 1024 * 1024


@functools.lru_cache(maxsize=None)
def circulant_blocks():
    table = np.zeros(PERIOD, np.float64)
    for n in range(1, PERIOD):
        if n != PERIOD // 2:
            sign = -1.0 if n % 2 else 1.0
            table[n] = math.pi / PERIOD * sign / math.tan(math.pi * n / PERIOD)
    row = np.arange(WIDE)
    offset = row[None, :] - row[:, None]
    return [table[(WIDE * d + offset) % PERIOD] for d in range(BLOCKS)]


def split_parts(parts):
    high = parts.astype(np.float32).astype(ml_dtypes.bfloat16)
    low = (parts - high.astype(np.float64)).astype(np.float32).astype(ml_dtypes.bfloat16)
    return np.stack([high, low], 1)


@functools.lru_cache(maxsize=None)
def residue_tables():
    dft = np.zeros((1, WIDE, 2 * WIDE), np.float64)
    cosines = [math.cos(2.0 * math.pi * n / WIDE) for n in range(WIDE)]
    sines = [math.sin(2.0 * math.pi * n / WIDE) for n in range(WIDE)]
    row = np.arange(WIDE)
    product = row[:, None] * row[None, :] % WIDE
    dft[0, :, :WIDE] = np.array(cosines)[product]
    dft[0, :, WIDE:] = -np.array(sines)[product]
    vectors = np.zeros((3, RES, WIDE), np.float64)
    for r in range(RES):
        for m in range(WIDE):
            turn = 2.0 * math.pi * (r * m) / PERIOD
            vectors[0, r, m], vectors[1, r, m] = math.cos(turn), math.sin(turn)
            freq = r + BLOCKS * m
            signed = freq if freq < PERIOD // 2 else freq - PERIOD
            if freq != PERIOD // 2:
                vectors[2, r, m] = 2.0 * math.pi * signed / PERIOD / PERIOD
    return split_parts(dft)[0], vectors.astype(np.float32)


def turned(value, turn):
    real, imag = value
    turn = turn % 1.0
    if turn == 0.0:
        return real, imag
    if turn == 0.5:
        return -real, (None if imag is None else -imag)
    if turn == 0.75:
        return imag, -real
    if turn == 0.25:
        return (None if imag is None else -imag), real
    cosine, sine = math.cos(2.0 * math.pi * turn), math.sin(2.0 * math.pi * turn)
    if imag is None:
        return real * cosine, real * sine
    return real * cosine - imag * sine, real * sine + imag * cosine


def plus(a, b):
    if b is None:
        return a
    return b if a is None else a + b


def minus(a, b):
    if b is None:
        return a
    return -b if a is None else a - b


def real_dft(values):
    count = len(values)
    if count == 2:
        return [(values[0] + values[1], None), (values[0] - values[1], None)]
    even, odd = real_dft(values[0::2]), real_dft(values[1::2])
    half, quarter = count // 2, count // 4
    result = [None] * (half + 1)
    for k in range(quarter + 1):
        spun = turned(odd[k], -k / count)
        result[k] = (plus(even[k][0], spun[0]), plus(even[k][1], spun[1]))
        mirror = (minus(even[k][0], spun[0]), minus(spun[1], even[k][1]))
        if k < quarter:
            result[half - k] = mirror
    return result


def real_inverse(spectrum):
    count = 2 * (len(spectrum) - 1)
    half, quarter = count // 2, count // 4
    if count == 2:
        return [spectrum[0][0] + spectrum[1][0], spectrum[0][0] - spectrum[1][0]]
    evens, odds = [], []
    for r in range(quarter + 1):
        low, high = spectrum[r], spectrum[half - r]
        total = (plus(low[0], high[0]), minus(low[1], high[1]))
        differ = (minus(low[0], high[0]), plus(low[1], high[1]))
        evens.append(total)
        odds.append(turned(differ, r / count))
    result = [None] * count
    result[0::2] = real_inverse(evens)
    result[1::2] = real_inverse(odds)
    return result


def store_split(target, first, second, value):
    high = value.astype(jnp.bfloat16)
    target[first] = high
    target[second] = (value - high.astype(jnp.float32)).astype(jnp.bfloat16)


def wide_product(lines, matrix):
    half = lines.shape[0] // 2
    main = jnp.dot(lines[...], matrix[0], preferred_element_type=jnp.float32)
    rest = jnp.dot(lines[:half], matrix[1], preferred_element_type=jnp.float32)
    both = main[:half] + main[half:] + rest
    quarter = half // 2
    return both[:quarter, :WIDE], both[:quarter, WIDE:], both[quarter:, :WIDE], both[quarter:, WIDE:]


def residue_part(some, residues, lines, matrix, vectors):
    def put(i, place, value):
        store_split(
            lines, pl.ds(96 * place + 32 * i, 32), pl.ds(192 + 96 * place + 32 * i, 32), value
        )

    for i, r in enumerate(some):
        cosine, sine = vectors[0, r : r + 1], vectors[1, r : r + 1]
        real, imag = residues[r, 0], residues[r, 1]
        put(i, 0, real * cosine + imag * sine)
        put(i, 1, imag * cosine - real * sine)
    rc, rs, ic, is_ = wide_product(lines, matrix)
    real, imag = rc - is_, rs + ic
    for i, r in enumerate(some):
        wave, at = vectors[2, r : r + 1], slice(32 * i, 32 * i + 32)
        put(i, 0, -wave * imag[at])
        put(i, 1, wave * real[at])
    rc, rs, ic, is_ = wide_product(lines, matrix)
    real, imag = rc + is_, ic - rs
    for i, r in enumerate(some):
        cosine, sine = vectors[0, r : r + 1], vectors[1, r : r + 1]
        at = slice(32 * i, 32 * i + 32)
        residues[r, 0] = real[at] * cosine - imag[at] * sine
        residues[r, 1] = real[at] * sine + imag[at] * cosine


def x_lines_kernel(lines_ref, after_ref, matrix, vectors, out_ref, work, residues, lines, sent):
    parts = [(pl.ds(16 * g, 16), pl.ds(128 * h, 128)) for g in range(2) for h in range(2)]
    outgoing = []
    for i, (rows, lanes) in enumerate(parts):
        here = (slice(None), rows, lanes)
        outgoing.append(pltpu.make_async_copy(work.at[here], out_ref.at[here], sent.at[i]))
        for r, (real, imag) in enumerate(real_dft([lines_ref[PLACE[p], rows, lanes] for p in range(BLOCKS)])):
            residues[r, 0, rows, lanes] = real
            residues[r, 1, rows, lanes] = jnp.zeros_like(real) if imag is None else imag
    for first in range(0, RES, 3):
        residue_part(range(first, first + 3), residues, lines, matrix, vectors)
    for copy, (rows, lanes) in zip(outgoing, parts):
        spectrum = []
        for r in range(RES):
            imag = None if r in (0, RES - 1) else residues[r, 1, rows, lanes]
            spectrum.append((residues[r, 0, rows, lanes], imag))
        for p, value in enumerate(real_inverse(spectrum)):
            work[PLACE[p], rows, lanes] = value
        copy.start()
    for copy in outgoing:
        copy.wait()


@functools.lru_cache(maxsize=None)
def ring_matrices():
    blocks = circulant_blocks()
    parts = np.zeros((16, WIDE, 4 * WIDE), np.float64)
    for own in range(4):
        for core in range(2):
            rows = slice(128 * core, 128 * core + 128)
            order = np.concatenate([np.arange(128) + 128 * core, np.arange(128) + 128 * (1 - core)])
            for k in range(4):
                target = parts[4 * own + 2 * core + k // 2, 128 * (k % 2) : 128 * (k % 2) + 128]
                for d in range(4):
                    block = blocks[(4 * d + own - (own - k) % 4) % BLOCKS][rows][:, order] / 4.0
                    target[:, :WIDE] += block
                    target[:, WIDE : 2 * WIDE] += block * (1 - 2 * (d % 2))
                    target[:, 2 * WIDE : 3 * WIDE] += 2.0 * block * (1, 0, -1, 0)[d]
                    target[:, 3 * WIDE :] -= 2.0 * block * (0, 1, 0, -1)[d]
    return split_parts(parts)


def load_kernel(me_ref, after_ref, matrix_ref, matrix, arrived):
    first = 2 * (me_ref[0] & 7)
    copy = pltpu.make_async_copy(matrix_ref.at[pl.ds(first, 2)], matrix, arrived)
    copy.start()
    copy.wait()


def ring_terms(pair, pieces, matrix, lines):
    for half, piece in enumerate(pieces):
        lanes = pl.ds(128 * half, 128)
        for group in range(16):
            at = pl.ds(16 * group, 16)
            w0, w1, w2, w3 = (piece[i, at, :] for i in (0, 3, 2, 1))
            values = (w0 + w2 + (w1 + w3), w0 + w2 - (w1 + w3), w0 - w2, w3 - w1)
            for value, offset, gap in zip(values, (0, 512, 1024, 1280), (256, 256, 512, 512)):
                store_split(
                    lines, (pl.ds(offset + 16 * group, 16), lanes), (pl.ds(offset + gap + 16 * group, 16), lanes), value
                )

    def product(offset, count, columns):
        main = jnp.dot(
            lines[offset : offset + 2 * count, :], matrix[pair, 0, :, columns], preferred_element_type=jnp.float32
        )
        rest = jnp.dot(
            lines[offset : offset + count, :], matrix[pair, 1, :, columns], preferred_element_type=jnp.float32
        )
        return main[:count] + main[count:] + rest

    both = product(1024, 512, slice(2 * WIDE, 4 * WIDE))
    return (
        product(0, 256, slice(0, WIDE)),
        product(512, 256, slice(WIDE, 2 * WIDE)),
        both[:256, :WIDE] - both[256:, WIDE:],
        both[:256, WIDE:] + both[256:, :WIDE],
    )


def y_first_kernel(p2, p3, matrix, sums, lines):
    for i, term in enumerate(ring_terms(1, (p2, p3), matrix, lines)):
        sums[i] = term


def y_lines_kernel(p0, p1, matrix, sums, own_ref, sent_ref, lines):
    z0, z2, real, imag = (sums[i] + term for i, term in enumerate(ring_terms(0, (p0, p1), matrix, lines)))
    for j, value in enumerate((z0 + z2 + real, z0 - z2 - imag, z0 + z2 - real, z0 - z2 + imag)):
        own_ref[j] = value[:, :128]
        sent_ref[j] = value[:, 128:]


def add_kernel(own_ref, other_ref, *out_refs):
    for j, out_ref in enumerate(out_refs):
        out_ref[...] = own_ref[j] + other_ref[j]


def whole(shape):
    return pl.BlockSpec(shape, lambda *_: (0,) * len(shape))


def any_place():
    return pl.BlockSpec(memory_space=pl.ANY)


def in_hbm():
    return pl.BlockSpec(memory_space=pltpu.HBM)


def in_vmem():
    return pl.BlockSpec(memory_space=pltpu.VMEM)


def in_smem():
    return pl.BlockSpec(memory_space=pltpu.SMEM)


def x_lines(lines, after):
    matrix, vectors = residue_tables()
    return pl.pallas_call(
        x_lines_kernel,
        in_specs=[in_vmem(), any_place(), in_vmem(), in_vmem()],
        out_specs=any_place(),
        out_shape=jax.ShapeDtypeStruct((BLOCKS, 32, WIDE), jnp.float32),
        scratch_shapes=[
            pltpu.VMEM((BLOCKS, 32, WIDE), jnp.float32),
            pltpu.VMEM((RES, 2, 32, WIDE), jnp.float32),
            pltpu.VMEM((384, WIDE), jnp.bfloat16),
            pltpu.SemaphoreType.DMA((4,)),
        ],
        cost_estimate=pl.CostEstimate(flops=900_000_000, bytes_accessed=1_000_000, transcendentals=0),
        compiler_params=pltpu.CompilerParams(vmem_limit_bytes=VMEM_LIMIT),
        name="x_lines",
    )(lines, after, jnp.asarray(matrix), jnp.asarray(vectors))


def load(me, after):
    matrices = ring_matrices()
    return pl.pallas_call(
        load_kernel,
        in_specs=[in_smem(), any_place(), in_hbm()],
        out_specs=in_vmem(),
        out_shape=jax.ShapeDtypeStruct((2,) + matrices.shape[1:], jnp.bfloat16),
        scratch_shapes=[pltpu.SemaphoreType.DMA],
        cost_estimate=pl.CostEstimate(flops=0, bytes_accessed=2_000_000, transcendentals=0),
        compiler_params=pltpu.CompilerParams(vmem_limit_bytes=VMEM_MOST),
        name="load",
    )(me, after, jnp.asarray(matrices))


def y_first(pieces, matrices):
    return pl.pallas_call(
        y_first_kernel,
        in_specs=[in_vmem()] * 3,
        out_specs=in_vmem(),
        out_shape=jax.ShapeDtypeStruct((4, 256, WIDE), jnp.float32),
        scratch_shapes=[pltpu.VMEM((2048, WIDE), jnp.bfloat16)],
        cost_estimate=pl.CostEstimate(flops=1_000_000_000, bytes_accessed=3_000_000, transcendentals=0),
        compiler_params=pltpu.CompilerParams(vmem_limit_bytes=VMEM_LIMIT),
        name="y_first",
    )(*pieces, matrices)


def y_lines(pieces, matrices, sums):
    half = jax.ShapeDtypeStruct((4, 256, 128), jnp.float32)
    return pl.pallas_call(
        y_lines_kernel,
        in_specs=[in_vmem()] * 4,
        out_specs=[in_vmem()] * 2,
        out_shape=[half] * 2,
        scratch_shapes=[pltpu.VMEM((2048, WIDE), jnp.bfloat16)],
        cost_estimate=pl.CostEstimate(flops=100_000_000_000, bytes_accessed=4_000_000, transcendentals=0),
        compiler_params=pltpu.CompilerParams(vmem_limit_bytes=VMEM_LIMIT),
        name="y_lines",
    )(*pieces, matrices, sums)


def add(own, other):
    return pl.pallas_call(
        add_kernel,
        in_specs=[in_vmem()] * 2,
        out_specs=[in_vmem()] * 4,
        out_shape=[jax.ShapeDtypeStruct((256, 128), jnp.float32)] * 4,
        cost_estimate=pl.CostEstimate(flops=200_000, bytes_accessed=1_500_000, transcendentals=0),
        compiler_params=pltpu.CompilerParams(vmem_limit_bytes=VMEM_LIMIT),
        name="add",
    )(own, other)


def pack_kernel(me_ref, fields, x_ref, q0, q1, q2, q3, lines, arrived):
    own_y = me_ref[0] >> 3
    copies = []
    for i in range(4):
        at = (slice(None), pl.ds(8 * i, 8))
        lines[at] = fields[i // 2 * 2, i % 2].T.reshape(16, 8, 256)
        copies.append(pltpu.make_async_copy(lines.at[at], x_ref.at[at], arrived.at[i]))
        copies[-1].start()
    for j, quarter in enumerate((q0, q1, q2, q3)):
        rows = pl.ds(pl.multiple_of(((own_y + j) & 3) * 64, 64), 64)
        for i in range(4):
            quarter[64 * i : 64 * i + 64, :] = fields[i // 2, i % 2, rows, :]
    for copy in copies:
        copy.wait()


def pack(me, fields):
    quarter = jax.ShapeDtypeStruct((256, 128), jnp.float32)
    return pl.pallas_call(
        pack_kernel,
        in_specs=[in_smem(), in_vmem()],
        out_specs=[any_place()] + [in_vmem()] * 4,
        out_shape=[jax.ShapeDtypeStruct((16, 32, 256), jnp.float32)] + [quarter] * 4,
        scratch_shapes=[pltpu.VMEM((16, 32, 256), jnp.float32), pltpu.SemaphoreType.DMA((4,))],
        cost_estimate=pl.CostEstimate(flops=0, bytes_accessed=2_000_000, transcendentals=0),
        compiler_params=pltpu.CompilerParams(vmem_limit_bytes=VMEM_LIMIT),
        name="pack",
    )(me, fields)


def shifted(value, axis, distance):
    pairs = []
    for i in range(32):
        at = [i // 8, i // 2 % 4, i % 2]
        at[axis] = (at[axis] + distance) % 4
        pairs.append((i, at[0] * 8 + at[1] * 2 + at[2]))
    return lax.ppermute(value, "gy", pairs)


def other_core(value):
    return lax.ppermute(value, "gy", [(i, i ^ 1) for i in range(32)])


def ring_swap(quarters):
    moved = {j: shifted(quarters[j], 0, j) for j in (1, 3, 2)}
    return [quarters[0]] + [moved[j] for j in (1, 2, 3)]


def ring_gather(held):
    moved = {j: shifted(held, 1, j) for j in (1, 3, 2)}
    return [held] + [moved[j] for j in (1, 2, 3)]


def base_kernel(
    fields_ref, poles_ref, stretch_ref, eps_ref, rates_ref, x_prof, y_prof, after_ref,
    next_poles, base, scale, vectors, fields, poles, stretch, inverse_eps, rates, out, arrived, sent
):
    pairs = [(poles_ref, poles), (rates_ref, rates), (fields_ref, fields), (eps_ref, inverse_eps), (stretch_ref, stretch)]
    copies = [pltpu.make_async_copy(a, b, arrived.at[k]) for k, (a, b) in enumerate(pairs)]
    for copy in copies:
        copy.start()
    conduct_x, stretch_x, shift_x = x_prof[0:1, :], x_prof[1:2, :], x_prof[2:3, :]
    conduct_y, stretch_y, shift_y = y_prof[0:1, :], y_prof[1:2, :], y_prof[2:3, :]
    decay_y = conduct_y / stretch_y + shift_y

    def down(row):
        return jnp.broadcast_to(row, (128, 256)).T

    decay_x = down(conduct_x / stretch_x + shift_x)
    vectors[0:1, :] = 1.0 / stretch_x
    vectors[1:2, :] = section_step * conduct_x / (stretch_x * stretch_x)
    vectors[2:3, 0:128] = 1.0 / stretch_y
    vectors[3:4, 0:128] = section_step * conduct_y / (stretch_y * stretch_y)
    for copy in copies[:3]:
        copy.wait()
    for plane in range(2):
        polar, current, ez = poles[0, plane], poles[1, plane], fields[0, plane]
        damping, resonance, plasma = (rates[i].astype(jnp.float32) for i in range(3))
        out[0, plane] = polar + section_step * current
        out[1, plane] = current + section_step * (plasma * ez - damping * current - resonance * polar)
    result = pltpu.make_async_copy(out, next_poles, sent)
    result.start()
    for copy in copies[3:]:
        copy.wait()
    eps = section_step * inverse_eps[...]
    scale[...] = eps
    for plane in range(2):
        s0, s1, s2, s3 = (stretch[i, plane] for i in range(4))
        base[0, plane] = fields[0, plane] + eps * (s1 - s3 - poles[1, plane])
        base[1, plane] = fields[1, plane] - section_step * s2
        base[2, plane] = fields[2, plane] + section_step * s0
        base[3, plane] = s0 - section_step * (decay_x * s0)
        base[4, plane] = s1 - section_step * (decay_x * s1)
        base[5, plane] = s2 - section_step * (decay_y * s2)
        base[6, plane] = s3 - section_step * (decay_y * s3)
    result.wait()


def base_part(fields, pole_state, stretch_state, inverse_permittivity, pole_rates, x_profile, y_profile, after):
    return pl.pallas_call(
        base_kernel,
        in_specs=[any_place()] * 5 + [in_vmem()] * 2 + [any_place()],
        out_specs=[in_hbm(), in_vmem(), in_vmem(), in_vmem()],
        out_shape=[
            jax.ShapeDtypeStruct((2, 2, 256, 128), jnp.float32),
            jax.ShapeDtypeStruct((7, 2, 256, 128), jnp.float32),
            jax.ShapeDtypeStruct((256, 128), jnp.float32),
            jax.ShapeDtypeStruct((8, 256), jnp.float32),
        ],
        scratch_shapes=[
            pltpu.VMEM((3, 2, 256, 128), jnp.float32),
            pltpu.VMEM((2, 2, 256, 128), jnp.float32),
            pltpu.VMEM((4, 2, 256, 128), jnp.float32),
            pltpu.VMEM((256, 128), jnp.float32),
            pltpu.VMEM((3, 256, 128), jnp.bfloat16),
            pltpu.VMEM((2, 2, 256, 128), jnp.float32),
            pltpu.SemaphoreType.DMA((5,)),
            pltpu.SemaphoreType.DMA,
        ],
        cost_estimate=pl.CostEstimate(flops=3_000_000, bytes_accessed=5_000_000, transcendentals=0),
        compiler_params=pltpu.CompilerParams(vmem_limit_bytes=VMEM_LIMIT),
        name="base",
    )(fields, pole_state, stretch_state, inverse_permittivity, pole_rates, x_profile, y_profile, after)


def finish_kernel(
    me_ref, base, scale, vectors, x_deriv, q0, q1, q2, q3, next_fields, next_stretch, fields, stretch, sent
):
    own_y = me_ref[0] >> 3
    over_y, feed_y = vectors[2:3, 0:128], vectors[3:4, 0:128]
    copies = []

    def send(source, target):
        copy = pltpu.make_async_copy(source, target, sent.at[len(copies)])
        copy.start()
        copies.append(copy)

    for plane in range(2):
        for j, quarter in enumerate((q0, q1, q2, q3)):
            rows = pl.ds(pl.multiple_of(((own_y - j) & 3) * 64, 64), 64)
            ez_dy = quarter[64 * plane : 64 * plane + 64, :]
            hx_dy = quarter[128 + 64 * plane : 192 + 64 * plane, :]
            stretch[2, plane, rows, :] = base[5, plane, rows, :] - feed_y * ez_dy
            stretch[3, plane, rows, :] = base[6, plane, rows, :] - feed_y * hx_dy
            fields[1, plane, rows, :] = base[1, plane, rows, :] - section_step * (over_y * ez_dy)
            fields[0, plane, rows, :] = base[0, plane, rows, :] - scale[rows, :] * (over_y * hx_dy)
        send(stretch.at[pl.ds(2, 2), plane], next_stretch.at[pl.ds(2, 2), plane])
        send(fields.at[1, plane], next_fields.at[1, plane])
    over_x, feed_x = (jnp.broadcast_to(vectors[i : i + 1, :], (128, 256)).T for i in range(2))
    eps = scale[...]
    for plane in range(2):
        ez_dx = x_deriv[:, 8 * plane : 8 * plane + 8, :].reshape(128, 256).T
        hy_dx = x_deriv[:, 16 + 8 * plane : 24 + 8 * plane, :].reshape(128, 256).T
        stretch[0, plane] = base[3, plane] - feed_x * ez_dx
        stretch[1, plane] = base[4, plane] - feed_x * hy_dx
        send(stretch.at[pl.ds(0, 2), plane], next_stretch.at[pl.ds(0, 2), plane])
        fields[2, plane] = base[2, plane] + section_step * (over_x * ez_dx)
        send(fields.at[2, plane], next_fields.at[2, plane])
        fields[0, plane] += eps * (over_x * hy_dx)
        send(fields.at[0, plane], next_fields.at[0, plane])
    for copy in copies:
        copy.wait()


def finish(me, base, scale, vectors, x_deriv, quarters):
    return pl.pallas_call(
        finish_kernel,
        in_specs=[in_smem()] + [in_vmem()] * 8,
        out_specs=[in_hbm()] * 2,
        out_shape=[jax.ShapeDtypeStruct((count, 2, 256, 128), jnp.float32) for count in (3, 4)],
        scratch_shapes=[
            pltpu.VMEM((3, 2, 256, 128), jnp.float32),
            pltpu.VMEM((4, 2, 256, 128), jnp.float32),
            pltpu.SemaphoreType.DMA((10,)),
        ],
        cost_estimate=pl.CostEstimate(flops=3_000_000, bytes_accessed=5_000_000, transcendentals=0),
        compiler_params=pltpu.CompilerParams(vmem_limit_bytes=VMEM_LIMIT),
        name="finish",
    )(me, base, scale, vectors, x_deriv, *quarters)


def swap_x(lines):
    return lax.all_to_all(lines, "gx", split_axis=0, concat_axis=0, tiled=True, axis_index_groups=[list(RING)])


def shards(fields, pole_state, stretch_state, inverse_permittivity, pole_rates, x_profile, y_profile):
    me = lax.axis_index("gy").astype(jnp.int32).reshape(1)
    x_packed, *y_packed = pack(me, fields)
    x_sorted = swap_x(x_packed)
    y_held = jnp.stack(ring_swap(y_packed))
    y_pieces = ring_gather(y_held)
    x_lined = x_lines(x_sorted, y_held)
    x_deriv = swap_x(x_lined)
    matrices = load(me, x_lined)
    own, sent = y_lines(y_pieces[:2], matrices, y_first(y_pieces[2:], matrices))
    y_lined = add(own, other_core(sent))
    next_poles, base, scale, vectors = base_part(
        fields, pole_state, stretch_state, inverse_permittivity, pole_rates, x_profile, y_profile, y_lined[0]
    )
    next_fields, next_stretch = finish(me, base, scale, vectors, x_deriv, ring_swap(y_lined))
    return next_fields, next_poles, next_stretch


def solution(mesh):
    return jax.shard_map(
        shards,
        mesh=mesh,
        in_specs=(
            P(None, None, "gx", "gy"),
            P(None, None, "gx", "gy"),
            P(None, None, "gx", "gy"),
            P("gx", "gy"),
            P(None, "gx", "gy"),
            P(None, "gx"),
            P(None, "gy"),
        ),
        out_specs=(P(None, None, "gx", "gy"), P(None, None, "gx", "gy"), P(None, None, "gx", "gy")),
        check_vma=False,
    )
```
